256 devices in a mesh: seq: 64 (over x, z, core), head: 4 (over y).
Axes of the slice: x: 4, y: 4, z: 8, core: 2. Of those that a mesh axis runs over, the one named last changes fastest.
Arguments:
- tokens: bfloat16 [65536, 1024], P('seq'), may hold values from -48 to 48
- cotangent: bfloat16 [65536, 1024], P('seq'), may hold values from -16 to 16
- w_query: bfloat16 [1024, 1024], P(None, 'head'), may hold values from -1 to 1
- w_key: bfloat16 [1024, 1024], P(None, 'head'), may hold values from -1 to 1
- w_value: bfloat16 [1024, 1024], P(None, 'head'), may hold values from -0.1875 to 0.1875
- w_out: bfloat16 [1024, 1024], P('head'), may hold values from -0.1875 to 0.1875
Outputs:
- layer_out: bfloat16 [65536, 1024], P('seq', 'head')
- grad_tokens: bfloat16 [65536, 1024], P('seq', 'head')
- grad_w_query: float32 [1024, 1024], P('seq', 'head')
- grad_w_key: float32 [1024, 1024], P('seq', 'head')
- grad_w_value: float32 [1024, 1024], P('seq', 'head')
- grad_w_out: float32 [1024, 1024], P('head', 'seq')
The draws below stay inside these ranges and needn't reach their ends.
All inputs are finite; a program needn't handle non-finite values.
Results may differ from the reference program's by a relative error of at most 0.017.
The reference program's roundings to bfloat16 on the way count: a program that leaves them out, or rounds other values in their place, can miss the bound.
Values may be sent and summed in bfloat16 or wider, within the bound.
No kernel may reach another device: no remote copies, remote signals or barrier semaphores. Data moves between devices by JAX's collectives and lax.ppermute only.
A program may use at most 192 MiB of HBM per device.

```python
import math
import jax
import jax.numpy as jnp
from jax import lax

D = 1024
HEAD_DIM = 64
BLOCK = 256
TOKENS = 65536
HEAD_COLS = 256
N_HEAD = 4


def shared_weight(key):
    return jax.random.normal(key, (D, D), jnp.float32) * D ** (-0.5)


def draw_w_query(key, part):
    common = shared_weight(key)
    return jnp.clip(common, -1.0, 1.0).astype(jnp.bfloat16)


def draw_w_key(key, part):
    key = jax.random.fold_in(key, 12)
    fresh_part = jax.random.normal(key, (D, D), jnp.float32) * D ** (-0.5)
    blended = fresh_part
    return jnp.clip(blended, -1.0, 1.0).astype(jnp.bfloat16)


def draw_tokens(key, part):
    key = jax.random.fold_in(key, 13)
    key_lead = jax.random.fold_in(key, 0)
    normal_rows = jax.random.normal(key_lead, (TOKENS, D), jnp.float32)
    result_rows = normal_rows
    return jnp.clip(result_rows, -48.0, 48.0).astype(jnp.bfloat16)


def strengthened(values, key, source, target, blocks, factor):
    owner, partner = [(jnp.arange(values.shape[position]) // (values.shape[position] // blocks)).reshape([-1 if axis == position else 1 for axis in range(values.ndim)]) for position in (source, target)]
    chosen = jax.random.permutation(key, blocks)[partner]
    strong = (owner == chosen) | (owner == (partner + blocks // 2) % blocks)
    return jnp.where(strong, factor * values, values)


def block_levels(stream_key, dims, pieces, least, largest):
    level, own = 1.0, jax.random.fold_in(stream_key, 6)
    for dim, parts in pieces:
        heights = jnp.exp(jax.random.uniform(jax.random.fold_in(own, dim), (parts,), jnp.float32, least / len(pieces), largest / len(pieces)))
        level = level * jnp.repeat(heights, dims[dim] // parts).reshape([-1 if axis == dim else 1 for axis in range(len(dims))])
    return level


def centred(own_key, dims, scale, limit, shards=(), held_as=jnp.bfloat16):
    gain = block_levels(own_key, dims, shards, -0.22, 0.18) if shards else 1.0
    entries = jax.random.normal(own_key, dims, jnp.float32) * scale * gain
    return jnp.minimum(jnp.maximum(entries, -limit), limit).astype(held_as)


def heavy_noise(stream_key, shape, width, bound, shards, heavy, held_as=jnp.bfloat16):
    result = width * jax.random.normal(stream_key, shape, jnp.float32)
    if shards:
        result = result * block_levels(stream_key, shape, shards, -0.22, 0.18)
    return jnp.clip(strengthened(result, jax.random.fold_in(stream_key, 3), *heavy), -bound, bound).astype(held_as)


def setup_inputs(seed: int = 0) -> dict:
    streams_of = jax.random.split(jax.random.key(seed), 7)
    return {
        "tokens": draw_tokens(jax.random.fold_in(streams_of[6], 71), 0),
        "cotangent": heavy_noise(streams_of[1], (TOKENS, D), 1.0, 16.0, ((0, 64),), (0, 1, 64, 4.0)),
        "w_query": draw_w_query(jax.random.fold_in(streams_of[6], 71), 0),
        "w_key": draw_w_key(jax.random.fold_in(streams_of[6], 71), 0),
        "w_value": centred(streams_of[4], (D, D), D ** -0.5, 0.1875, ((1, 4),)),
        "w_out": centred(streams_of[5], (D, D), D ** -0.5, 0.1875, ((0, 4),)),
    }


def product(former, latter):
    return jnp.dot(former, latter, preferred_element_type=jnp.float32)

def contract_rows(former, latter):
    return lax.dot_general(former, latter, (((0,), (0,)), ((), ())), preferred_element_type=jnp.float32)

def contract_cols(former, latter):
    return lax.dot_general(former, latter, (((1,), (1,)), ((), ())), preferred_element_type=jnp.float32)

def coarsen(key_rows, factor):
    grouped = key_rows.astype(jnp.float32).reshape(key_rows.shape[0] // factor, factor, key_rows.shape[1])
    return (lax.optimization_barrier(jnp.sum(grouped, axis=1)) * (1.0 / factor)).astype(jnp.bfloat16)

def expand(coarse_rows, factor):
    return jnp.repeat(coarse_rows, factor, axis=0) * (1.0 / factor)

def key_offsets():
    return jnp.concatenate([jnp.zeros((2 * BLOCK,), jnp.float32), jnp.full((BLOCK,), math.log(2.0), jnp.float32), jnp.full((BLOCK,), math.log(4.0), jnp.float32), jnp.full((BLOCK,), math.log(8.0), jnp.float32)])

def gather_keys(key_value, half_index, level_two, level_three):
    pair_span = 2 * BLOCK
    near_rows = key_value[half_index * pair_span:(half_index + 1) * pair_span]
    far_rows = key_value[(1 - half_index) * pair_span:(2 - half_index) * pair_span]
    return jnp.concatenate([near_rows, coarsen(far_rows, 2), level_two, level_three], axis=0)

def split_heads(matrix):
    return matrix.astype(jnp.float32).reshape(matrix.shape[0], matrix.shape[1] // HEAD_DIM, HEAD_DIM)

def probabilities(part_query, key_rows, offsets):
    scores = jnp.einsum('qhd,khd->hqk', split_heads(part_query), split_heads(key_rows))
    scores = scores * (1.0 / math.sqrt(HEAD_DIM)) + offsets
    row_max = lax.optimization_barrier(jnp.max(scores, axis=-1, keepdims=True))
    raised = jnp.exp(scores - row_max)
    return raised / lax.optimization_barrier(jnp.sum(raised, axis=-1, keepdims=True))

def group_forward(queries, key_value, level_two, level_three):
    feature_width = queries.shape[1]
    pair_span = 2 * BLOCK
    offsets = key_offsets()
    outputs = []
    for half_index in range(2):
        key_rows = gather_keys(key_value, half_index, level_two, level_three)
        part_query = queries[half_index * pair_span:(half_index + 1) * pair_span]
        attention = probabilities(part_query, key_rows[:, :feature_width], offsets)
        weights = attention.astype(jnp.bfloat16)
        blended = jnp.einsum('hqk,khd->qhd', weights.astype(jnp.float32), split_heads(key_rows[:, feature_width:]))
        outputs.append(blended.reshape(pair_span, feature_width))
    return jnp.concatenate(outputs, axis=0).astype(jnp.bfloat16)

def attention_grads(attention, part_query, key_rows, part_grad, feature_width):
    query_count = part_query.shape[0]
    key_count = key_rows.shape[0]
    query_heads = split_heads(part_query)
    key_heads = split_heads(key_rows[:, :feature_width])
    value_heads = split_heads(key_rows[:, feature_width:])
    grad_heads = split_heads(part_grad)
    weights = attention.astype(jnp.bfloat16).astype(jnp.float32)
    grad_attention = jnp.einsum('qhd,khd->hqk', grad_heads, value_heads)
    row_inner = lax.optimization_barrier(jnp.sum(attention * grad_attention, axis=-1, keepdims=True))
    grad_scores = (attention * (grad_attention - row_inner) * (1.0 / math.sqrt(HEAD_DIM))).astype(jnp.bfloat16)
    grad_scores = grad_scores.astype(jnp.float32)
    grad_query = jnp.einsum('hqk,khd->qhd', grad_scores, key_heads).reshape(query_count, feature_width)
    grad_keys = jnp.einsum('hqk,qhd->khd', grad_scores, query_heads).reshape(key_count, feature_width)
    grad_values = jnp.einsum('hqk,qhd->khd', weights, grad_heads).reshape(key_count, feature_width)
    return (grad_query, jnp.concatenate([grad_keys, grad_values], axis=1))

def group_backward(queries, key_value, level_two, level_three, d_attended):
    feature_width = queries.shape[1]
    pair_span = 2 * BLOCK
    offsets = key_offsets()
    halves = []
    for half_index in range(2):
        key_rows = gather_keys(key_value, half_index, level_two, level_three)
        part_query = queries[half_index * pair_span:(half_index + 1) * pair_span]
        part_grad = d_attended[half_index * pair_span:(half_index + 1) * pair_span]
        attention = probabilities(part_query, key_rows[:, :feature_width], offsets)
        halves.append(attention_grads(attention, part_query, key_rows, part_grad, feature_width))
    first_half = halves[0][1]
    second_half = halves[1][1]
    grad_query = jnp.concatenate([halves[0][0], halves[1][0]], axis=0)
    grad_own = jnp.concatenate([first_half[:pair_span] + expand(second_half[pair_span:pair_span + BLOCK], 2), second_half[:pair_span] + expand(first_half[pair_span:pair_span + BLOCK], 2)], axis=0)
    grad_two = first_half[pair_span + BLOCK:pair_span + 2 * BLOCK] + second_half[pair_span + BLOCK:pair_span + 2 * BLOCK]
    grad_three = first_half[pair_span + 2 * BLOCK:] + second_half[pair_span + 2 * BLOCK:]
    return (grad_query, grad_own, grad_two, grad_three)

def reference(tokens, cotangent, w_query, w_key, w_value, w_out):
    queries = product(tokens, w_query).astype(jnp.bfloat16)
    key_proj = product(tokens, w_key).astype(jnp.bfloat16)
    values = product(tokens, w_value).astype(jnp.bfloat16)
    key_value = jnp.concatenate([key_proj, values], axis=1)
    level_two_all = coarsen(key_value, 4)
    level_three_all = coarsen(key_value, 8)
    group_rows = 4 * BLOCK
    group_total = TOKENS // group_rows
    full_width = 2 * D
    indices = jnp.arange(group_total, dtype=jnp.int32)

    def inputs_of(group_index):
        row_start = (group_index * group_rows).astype(jnp.int32)
        own_query = lax.dynamic_slice_in_dim(queries, row_start, group_rows, 0)
        own_key_value = lax.dynamic_slice_in_dim(key_value, row_start, group_rows, 0)
        sibling_two = (jnp.bitwise_xor(group_index, 1) * BLOCK).astype(jnp.int32)
        sibling_three = (jnp.bitwise_xor(group_index // 2, 1) * BLOCK).astype(jnp.int32)
        level_two = lax.dynamic_slice_in_dim(level_two_all, sibling_two, BLOCK, 0)
        level_three = lax.dynamic_slice_in_dim(level_three_all, sibling_three, BLOCK, 0)
        return (own_query, own_key_value, level_two, level_three, row_start)

    def forward_group(group_index):
        own_query, own_key_value, level_two, level_three, row_start = inputs_of(group_index)
        return group_forward(own_query, own_key_value, level_two, level_three)
    attended = lax.map(forward_group, indices).reshape(TOKENS, D)
    layer_total = jnp.zeros((TOKENS, D), jnp.float32)
    for head_group in range(N_HEAD):
        col_start = head_group * HEAD_COLS
        col_stop = col_start + HEAD_COLS
        partial_value = product(attended[:, col_start:col_stop], w_out[col_start:col_stop]).astype(jnp.bfloat16)
        layer_total = layer_total + lax.optimization_barrier(partial_value).astype(jnp.float32)
    layer_out = layer_total.astype(jnp.bfloat16)
    d_attended = contract_cols(cotangent, w_out).astype(jnp.bfloat16)

    def backward_group(group_index):
        own_query, own_key_value, level_two, level_three, row_start = inputs_of(group_index)
        own_grad = lax.dynamic_slice_in_dim(d_attended, row_start, group_rows, 0)
        return group_backward(own_query, own_key_value, level_two, level_three, own_grad)
    grad_query, grad_own, grad_two, grad_three = lax.map(backward_group, indices)
    got_two = jnp.flip(grad_two.reshape(group_total // 2, 2, BLOCK, full_width), axis=1)
    got_two = got_two.reshape(group_total, BLOCK, full_width)
    pair_sums = lax.optimization_barrier(jnp.sum(grad_three.reshape(group_total // 4, 2, 2, BLOCK, full_width), axis=2))
    got_three = jnp.flip(pair_sums, axis=1).reshape(group_total, BLOCK // 2, full_width)
    grad_key_value = grad_own + jnp.repeat(got_two, 4, axis=1) * 0.25 + jnp.repeat(got_three, 8, axis=1) * 0.125
    grad_key_value = grad_key_value.reshape(TOKENS, full_width)
    query_grad = grad_query.reshape(TOKENS, D).astype(jnp.bfloat16)
    key_grad = grad_key_value[:, :D].astype(jnp.bfloat16)
    value_grad = grad_key_value[:, D:].astype(jnp.bfloat16)
    input_total = jnp.zeros((TOKENS, D), jnp.float32)
    for head_group in range(N_HEAD):
        col_start = head_group * HEAD_COLS
        col_stop = col_start + HEAD_COLS
        partial_value = contract_cols(query_grad[:, col_start:col_stop], w_query[:, col_start:col_stop])
        partial_value = partial_value + contract_cols(key_grad[:, col_start:col_stop], w_key[:, col_start:col_stop])
        partial_value = partial_value + contract_cols(value_grad[:, col_start:col_stop], w_value[:, col_start:col_stop])
        partial_value = partial_value.astype(jnp.bfloat16)
        input_total = input_total + lax.optimization_barrier(partial_value).astype(jnp.float32)
    grad_tokens = input_total.astype(jnp.bfloat16)
    grad_scale = 1.0 / math.sqrt(TOKENS)
    grad_w_query = contract_rows(tokens, query_grad) * grad_scale
    grad_w_key = contract_rows(tokens, key_grad) * grad_scale
    grad_w_value = contract_rows(tokens, value_grad) * grad_scale
    grad_w_out = contract_rows(attended, cotangent) * grad_scale
    return (layer_out, grad_tokens, grad_w_query, grad_w_key, grad_w_value, grad_w_out)
```

```python
import functools
import math

import jax
import jax.numpy as jnp
from jax import lax
from jax.experimental import pallas as pl
from jax.experimental.pallas import tpu as pltpu
from jax.sharding import PartitionSpec as P

HEAD_DIM = 64
BLOCK = 256
SPAN = 2 * BLOCK
KEYS = 5 * BLOCK
ROWS = 4 * BLOCK
WIDTH = 1024
COLS = 256
MIB = 1024 * 1024
OFFSETS = (0.0, 0.0, 1.0, 2.0, 3.0)
SCORE_SCALE = 1.0 / (math.log(2.0) * math.sqrt(HEAD_DIM))
INV_ROOT = 1.0 / math.sqrt(HEAD_DIM)
bf16 = jnp.bfloat16
f32 = jnp.float32


def dot_nn(a, b):
    return lax.dot_general(a, b, (((1,), (0,)), ((), ())), preferred_element_type=f32)


def dot_nt(a, b):
    return lax.dot_general(a, b, (((1,), (1,)), ((), ())), preferred_element_type=f32)


def params(mib):
    return pltpu.CompilerParams(vmem_limit_bytes=mib * MIB)


def shape(dims, dtype=bf16):
    return jax.ShapeDtypeStruct(dims, dtype)


def cost(macs, nbytes):
    return pl.CostEstimate(flops=2 * macs, bytes_accessed=nbytes, transcendentals=0)


def run_matrix(rows, cols, shift, expand):
    i = lax.broadcasted_iota(jnp.int32, (rows, cols), 0)
    j = lax.broadcasted_iota(jnp.int32, (rows, cols), 1)
    inside = (i >> shift) == j if expand else i == (j >> shift)
    return jnp.where(inside, 2.0**-shift, 0.0).astype(bf16)


def kv_kernel(x_ref, wk_ref, wv_ref, kv_ref, c2_ref, c4_ref, c8_ref):
    x = x_ref[...]
    kv_ref[:, :COLS] = dot_nn(x, wk_ref[...]).astype(bf16)
    kv_ref[:, COLS:] = dot_nn(x, wv_ref[...]).astype(bf16)
    kv = kv_ref[...]
    for shift, ref in ((1, c2_ref), (2, c4_ref), (3, c8_ref)):
        average = run_matrix(BLOCK >> shift, BLOCK, shift, False)
        ref[...] = dot_nn(average, kv).astype(bf16)


def project_kv(tokens, w_key, w_value):
    whole = pl.BlockSpec((WIDTH, COLS), lambda i: (0, 0))
    return pl.pallas_call(
        kv_kernel,
        grid=(4,),
        in_specs=[pl.BlockSpec((BLOCK, WIDTH), lambda i: (i, 0)), whole, whole],
        out_specs=[pl.BlockSpec((BLOCK >> s, 2 * COLS), lambda i: (i, 0)) for s in range(4)],
        out_shape=[shape((ROWS >> s, 2 * COLS)) for s in range(4)],
        compiler_params=params(24),
        cost_estimate=cost(ROWS * WIDTH * 2 * COLS, 6 * MIB),
        name="project_kv",
    )(tokens, w_key, w_value)


def q_kernel(x_ref, c_ref, wq_ref, wo_ref, q_ref, da_ref):
    q_ref[...] = dot_nn(x_ref[...], wq_ref[...]).astype(bf16)
    da_ref[...] = dot_nt(c_ref[...], wo_ref[...]).astype(bf16)


def project_q(tokens, cotangent, w_query, w_out):
    rows = pl.BlockSpec((BLOCK, WIDTH), lambda i: (i, 0))
    out = pl.BlockSpec((BLOCK, COLS), lambda i: (i, 0))
    return pl.pallas_call(
        q_kernel,
        grid=(4,),
        in_specs=[
            rows,
            rows,
            pl.BlockSpec((WIDTH, COLS), lambda i: (0, 0)),
            pl.BlockSpec((COLS, WIDTH), lambda i: (0, 0)),
        ],
        out_specs=[out, out],
        out_shape=[shape((ROWS, COLS))] * 2,
        compiler_params=params(24),
        cost_estimate=cost(ROWS * WIDTH * 2 * COLS, 7 * MIB),
        name="project_q",
    )(tokens, cotangent, w_query, w_out)


def entry_rows(refs, kb, lo):
    near, c2, l2, l3a, l3b = refs
    if kb < 2:
        return near[kb * BLOCK : (kb + 1) * BLOCK, lo : lo + 128]
    if kb == 2:
        return c2[:, lo : lo + 128]
    if kb == 3:
        return l2[:, lo : lo + 128]
    return jnp.concatenate([l3a[:, lo : lo + 128], l3b[:, lo : lo + 128]], axis=0)


def only_head(ref, head):
    lane = lax.broadcasted_iota(jnp.int32, (SPAN, 128), 1)
    keep = lane < HEAD_DIM if head % 2 == 0 else lane >= HEAD_DIM
    pair = head // 2 * 128
    return jnp.where(keep, ref[:, pair : pair + 128], jnp.zeros((), bf16))


def fold(values, combine):
    return combine(values.reshape(BLOCK // 8, 8, SPAN), axis=0)


def forward_kernel(*refs):
    entries, q_ref, ot_ref, stat_ref = refs[:5], refs[5], refs[6], refs[7]
    t_s, vt_s, qm_s = refs[8:]
    for kb in range(5):
        rows = slice(kb * BLOCK, (kb + 1) * BLOCK)
        for pair in range(2):
            vt_s[pair * 128 : pair * 128 + 128, rows] = entry_rows(
                entries, kb, COLS + pair * 128
            ).T
    for head in range(4):
        qm_s[head] = only_head(q_ref, head)
    for head in range(4):
        lo = head // 2 * 128
        slot = head % 2
        tops = []
        for kb in range(5):
            rows = slice(kb * BLOCK, (kb + 1) * BLOCK)
            t = dot_nt(entry_rows(entries, kb, lo), qm_s[head]) * SCORE_SCALE
            t_s[slot, rows] = t
            tops.append(fold(t, jnp.max) + OFFSETS[kb])
        top = jnp.max(functools.reduce(jnp.maximum, tops), axis=0, keepdims=True)
        total = jnp.zeros((8, SPAN), f32)
        for kb in range(5):
            rows = slice(kb * BLOCK, (kb + 1) * BLOCK)
            raised = jnp.exp2(t_s[slot, rows] + (OFFSETS[kb] - top))
            t_s[slot, rows] = raised
            total = total + fold(raised, jnp.sum)
        total = jnp.sum(total, axis=0, keepdims=True)
        inverse = 1.0 / total
        out = jnp.zeros((HEAD_DIM, SPAN), f32)
        mine = slice(head * HEAD_DIM, (head + 1) * HEAD_DIM)
        for kb in range(5):
            rows = slice(kb * BLOCK, (kb + 1) * BLOCK)
            weights = (t_s[slot, rows] * inverse).astype(bf16)
            out = out + dot_nn(vt_s[mine, rows], weights)
        ot_ref[mine] = out.astype(bf16)
        stat_ref[head : head + 1] = top
        stat_ref[head + 4 : head + 5] = inverse


def entry_specs():
    return [
        pl.BlockSpec((SPAN, 2 * COLS), lambda i: (i, 0)),
        pl.BlockSpec((BLOCK, 2 * COLS), lambda i: (1 - i, 0)),
        pl.BlockSpec((BLOCK, 2 * COLS), lambda i: (0, 0)),
        pl.BlockSpec((BLOCK // 2, 2 * COLS), lambda i: (0, 0)),
        pl.BlockSpec((BLOCK // 2, 2 * COLS), lambda i: (0, 0)),
    ]


def attend(entries, queries):
    return pl.pallas_call(
        forward_kernel,
        grid=(2,),
        in_specs=entry_specs() + [pl.BlockSpec((SPAN, COLS), lambda i: (i, 0))],
        out_specs=[
            pl.BlockSpec((COLS, SPAN), lambda i: (0, i)),
            pl.BlockSpec((8, SPAN), lambda i: (0, i)),
        ],
        out_shape=[shape((COLS, ROWS)), shape((8, ROWS), f32)],
        scratch_shapes=[
            pltpu.VMEM((2, KEYS, SPAN), f32),
            pltpu.VMEM((COLS, KEYS), bf16),
            pltpu.VMEM((4, SPAN, 128), bf16),
        ],
        compiler_params=params(40),
        cost_estimate=cost(4 * 2 * 4 * ROWS * KEYS * 64, 4 * MIB),
        name="attend",
    )(*entries, queries)


def split_product(matrix, values):
    high = values.astype(bf16)
    low = (values - high.astype(f32)).astype(bf16)
    return dot_nn(matrix, high) + dot_nn(matrix, low)


def backward_kernel(*refs):
    entries, q_ref, da_ref, stat_ref = refs[:5], refs[5], refs[6], refs[7]
    qgt_ref, own_ref, g2_ref, g3_ref = refs[8:12]
    a_s, p_s, kt_s, qm_s, dm_s, grad_s, far_s = refs[12:]
    for kb in range(5):
        rows = slice(kb * BLOCK, (kb + 1) * BLOCK)
        for pair in range(2):
            kt_s[pair * 128 : pair * 128 + 128, rows] = entry_rows(entries, kb, pair * 128).T
    for head in range(4):
        qm_s[head] = only_head(q_ref, head)
        dm_s[head] = only_head(da_ref, head)
    for head in range(4):
        lo = head // 2 * 128
        slot = head % 2
        top = stat_ref[head : head + 1]
        inverse = stat_ref[head + 4 : head + 5]
        inner = jnp.zeros((8, SPAN), f32)
        for kb in range(5):
            rows = slice(kb * BLOCK, (kb + 1) * BLOCK)
            t = dot_nt(entry_rows(entries, kb, lo), qm_s[head]) * SCORE_SCALE
            a = jnp.exp2(t + (OFFSETS[kb] - top)) * inverse
            p = dot_nt(entry_rows(entries, kb, COLS + lo), dm_s[head])
            a_s[slot, rows] = a
            p_s[slot, rows] = p
            inner = inner + fold(a * p, jnp.sum)
        inner = jnp.sum(inner, axis=0, keepdims=True)
        query_grad = jnp.zeros((HEAD_DIM, SPAN), f32)
        mine = slice(head * HEAD_DIM, (head + 1) * HEAD_DIM)
        for kb in range(5):
            rows = slice(kb * BLOCK, (kb + 1) * BLOCK)
            a = a_s[slot, rows]
            weights = a.astype(bf16)
            scores = (a * (p_s[slot, rows] - inner)).astype(bf16)
            query_grad = query_grad + dot_nn(kt_s[mine, rows], scores)
            dk = dot_nn(scores, qm_s[head])
            dv = dot_nn(weights, dm_s[head])
            if head % 2 == 0:
                grad_s[rows, lo : lo + 128] = dk
                grad_s[rows, COLS + lo : COLS + lo + 128] = dv
            else:
                dk = (grad_s[rows, lo : lo + 128] + dk) * INV_ROOT
                grad_s[rows, lo : lo + 128] = dk
                grad_s[rows, COLS + lo : COLS + lo + 128] += dv
        qgt_ref[mine] = (query_grad * INV_ROOT).astype(bf16)
    spread = run_matrix(SPAN, BLOCK, 1, True)
    sibling = split_product(spread, grad_s[SPAN : SPAN + BLOCK])

    @pl.when(pl.program_id(0) == 0)
    def _():
        own_ref[:SPAN] = grad_s[:SPAN]
        own_ref[SPAN:] = sibling
        far_s[...] = grad_s[SPAN + BLOCK :]

    @pl.when(pl.program_id(0) == 1)
    def _():
        own_ref[:SPAN] += sibling
        own_ref[SPAN:] += grad_s[:SPAN]
        g2_ref[...] = (far_s[:BLOCK] + grad_s[SPAN + BLOCK : SPAN + 2 * BLOCK]).astype(bf16)
        g3_ref[...] = (far_s[BLOCK:] + grad_s[SPAN + 2 * BLOCK :]).astype(bf16)


def attend_grads(entries, queries, d_attended, stats):
    part = pl.BlockSpec((SPAN, COLS), lambda i: (i, 0))
    coarse = pl.BlockSpec((BLOCK, 2 * COLS), lambda i: (0, 0))
    return pl.pallas_call(
        backward_kernel,
        grid=(2,),
        in_specs=entry_specs() + [part, part, pl.BlockSpec((8, SPAN), lambda i: (0, i))],
        out_specs=[
            pl.BlockSpec((COLS, SPAN), lambda i: (0, i)),
            pl.BlockSpec((ROWS, 2 * COLS), lambda i: (0, 0)),
            coarse,
            coarse,
        ],
        out_shape=[
            shape((COLS, ROWS)),
            shape((ROWS, 2 * COLS), f32),
            shape((BLOCK, 2 * COLS)),
            shape((BLOCK, 2 * COLS)),
        ],
        scratch_shapes=[
            pltpu.VMEM((2, KEYS, SPAN), f32),
            pltpu.VMEM((2, KEYS, SPAN), f32),
            pltpu.VMEM((COLS, KEYS), bf16),
            pltpu.VMEM((4, SPAN, 128), bf16),
            pltpu.VMEM((4, SPAN, 128), bf16),
            pltpu.VMEM((KEYS, 2 * COLS), f32),
            pltpu.VMEM((2 * BLOCK, 2 * COLS), f32),
        ],
        compiler_params=params(48),
        cost_estimate=cost(4 * 5 * 4 * ROWS * KEYS * 64, 8 * MIB),
        name="attend_grads",
    )(*entries, queries, d_attended, stats)


def ring_columns(step):
    first = step < 2
    return jnp.where(first, 2, 1), jnp.where(first, 3, 2), jnp.where(first, 1, 3)


def ring_specs():
    spec = pl.BlockSpec((BLOCK, COLS), lambda i, s: (i, 0))
    return [spec] * 4, [shape((ROWS, COLS))] * 4


def out_kernel(at_ref, ot_ref, w_ref, right_ref, left_ref, hold_ref, mine_ref):
    step = pl.program_id(0)
    here = at_ref[0]
    rows = ot_ref[...].T
    for offset, ref in zip(ring_columns(step) + (0,), (right_ref, left_ref, hold_ref, mine_ref)):
        start = pl.multiple_of(((here + offset) & 3) * COLS, COLS)
        ref[...] = dot_nn(rows, w_ref[:, pl.ds(start, COLS)]).astype(bf16)


def project_out(at, attended_t, w_out):
    out_specs, out_shape = ring_specs()
    return pl.pallas_call(
        out_kernel,
        grid_spec=pltpu.PrefetchScalarGridSpec(
            num_scalar_prefetch=1,
            grid=(4,),
            in_specs=[
                pl.BlockSpec((COLS, BLOCK), lambda i, s: (0, i)),
                pl.BlockSpec((COLS, WIDTH), lambda i, s: (0, 0)),
            ],
            out_specs=out_specs,
        ),
        out_shape=out_shape,
        compiler_params=params(24),
        cost_estimate=cost(ROWS * WIDTH * COLS, 4 * MIB),
        name="project_out",
    )(at, attended_t, w_out)


def input_kernel(
    at_ref, own_ref, got2_ref, got3a_ref, got3b_ref, qgt_ref, wq_ref, wk_ref, wv_ref,
    right_ref, left_ref, hold_ref, mine_ref, kvg_ref,
):
    step = pl.program_id(0)
    here = at_ref[0]
    spread4 = run_matrix(BLOCK, BLOCK >> 2, 2, True)
    spread8 = run_matrix(BLOCK, BLOCK >> 3, 3, True)
    total = own_ref[...] + dot_nn(spread4, got2_ref[...])
    total = total + (dot_nn(spread8, got3a_ref[...]) + dot_nn(spread8, got3b_ref[...]))
    kvg = total.astype(bf16)
    kvg_ref[...] = kvg
    query_grad = qgt_ref[...].T
    for offset, ref in zip(ring_columns(step) + (0,), (right_ref, left_ref, hold_ref, mine_ref)):
        start = pl.multiple_of(((here + offset) & 3) * COLS, COLS)
        cols = pl.ds(start, COLS)
        part = dot_nt(query_grad, wq_ref[cols, :])
        part = part + dot_nt(kvg[:, :COLS], wk_ref[cols, :])
        part = part + dot_nt(kvg[:, COLS:], wv_ref[cols, :])
        ref[...] = part.astype(bf16)


def project_input(at, own, got2, got3a, got3b, query_grad_t, w_query, w_key, w_value):
    out_specs, out_shape = ring_specs()
    whole = pl.BlockSpec((WIDTH, COLS), lambda i, s: (0, 0))
    return pl.pallas_call(
        input_kernel,
        grid_spec=pltpu.PrefetchScalarGridSpec(
            num_scalar_prefetch=1,
            grid=(4,),
            in_specs=[
                pl.BlockSpec((BLOCK, 2 * COLS), lambda i, s: (i, 0)),
                pl.BlockSpec((BLOCK >> 2, 2 * COLS), lambda i, s: (i, 0)),
                pl.BlockSpec((BLOCK >> 3, 2 * COLS), lambda i, s: (i, 0)),
                pl.BlockSpec((BLOCK >> 3, 2 * COLS), lambda i, s: (i, 0)),
                pl.BlockSpec((COLS, BLOCK), lambda i, s: (0, i)),
                whole,
                whole,
                whole,
            ],
            out_specs=out_specs + [pl.BlockSpec((BLOCK, 2 * COLS), lambda i, s: (i, 0))],
        ),
        out_shape=out_shape + [shape((ROWS, 2 * COLS))],
        compiler_params=params(32),
        cost_estimate=cost(3 * ROWS * WIDTH * COLS, 8 * MIB),
        name="project_input",
    )(at, own, got2, got3a, got3b, query_grad_t, w_query, w_key, w_value)


def shifted(value, axis, by):
    size = lax.axis_size(axis)
    return lax.ppermute(value, axis, [(i, (i + by) % size) for i in range(size)])


def swapped(value, bits):
    return lax.ppermute(value, "seq", [(i, i ^ bits) for i in range(lax.axis_size("seq"))])


def add(*terms):
    return sum(term.astype(f32) for term in terms).astype(bf16)


def head_sum(right, left, hold, mine):
    half = ROWS // 2
    got_right = shifted(right, "head", 1)
    got_left = shifted(left, "head", -1)
    more_right = shifted(add(hold[:half], got_right[:half]), "head", 1)
    more_left = shifted(add(hold[half:], got_left[half:]), "head", -1)
    return jnp.concatenate(
        [
            add(mine[:half], got_left[:half], more_right),
            add(mine[half:], got_right[half:], more_left),
        ],
        axis=0,
    )


def weight_kernel(at_ref, x_ref, c_ref, ot_ref, qgt_ref, kvg_ref, mine_ref, other_ref, g_s):
    core = at_ref[1]
    for index in range(4):
        if index == 0:
            grad_t = dot_nn(qgt_ref[...], x_ref[...])
        elif index < 3:
            cols = kvg_ref[:, (index - 1) * COLS : index * COLS]
            grad_t = dot_nn(cols.T, x_ref[...])
        else:
            grad_t = dot_nn(ot_ref[...], c_ref[...])
        g_s[...] = grad_t.astype(bf16).T.reshape(64, 16, COLS)
        rows = slice(index * 16, (index + 1) * 16)
        for block in range(32):
            mine_ref[block, rows] = g_s[2 * block + core]
            other_ref[block, rows] = g_s[2 * block + 1 - core]


def weight_grads(at, tokens, cotangent, attended_t, query_grad_t, kv_grad):
    vmem = pl.BlockSpec(memory_space=pltpu.VMEM)
    return pl.pallas_call(
        weight_kernel,
        in_specs=[pl.BlockSpec(memory_space=pltpu.SMEM)] + [vmem] * 5,
        out_specs=[vmem] * 2,
        out_shape=[shape((32, 64, COLS))] * 2,
        scratch_shapes=[pltpu.VMEM((64, 16, COLS), bf16)],
        compiler_params=params(40),
        cost_estimate=cost(4 * ROWS * WIDTH * COLS, 8 * MIB),
        name="weight_grads",
    )(at, tokens, cotangent, attended_t, query_grad_t, kv_grad)


def stage_kernel(at_ref, kept_ref, got_ref, *outs, picks):
    total_s = outs[-1]
    total_s[...] = (kept_ref[...].astype(f32) + got_ref[...].astype(f32)).astype(bf16)
    for pick, ref in zip(picks, outs[:-1]):
        for block, source in enumerate(pick(at_ref)):
            ref[block] = total_s[source]


def stage(at, kept, got, picks, counts, name):
    vmem = pl.BlockSpec(memory_space=pltpu.VMEM)
    rest = kept.shape[1:]
    return pl.pallas_call(
        functools.partial(stage_kernel, picks=picks),
        in_specs=[pl.BlockSpec(memory_space=pltpu.SMEM)] + [vmem] * 2,
        out_specs=[vmem] * len(counts),
        out_shape=[shape((count, *rest)) for count in counts],
        scratch_shapes=[pltpu.VMEM(kept.shape, bf16)],
        compiler_params=params(24),
        name=name,
    )(at, kept, got)


def x_blocks(offset, first, count):
    return lambda at: [((at[2] + offset) & 3) * 8 + first + block for block in range(count)]


def z_blocks(bit, count, flip):
    def pick(at):
        mine = (at[3] >> bit) & 1
        return [2 * block + (1 - mine if flip else mine) for block in range(count)]

    return pick


def seq_sum(at, mine, other):
    got = swapped(other, 1)
    far_a, far_b, ahead, behind, here = stage(
        at,
        mine,
        got,
        [x_blocks(2, 0, 4), x_blocks(2, 4, 4), x_blocks(1, 0, 8), x_blocks(3, 0, 8)]
        + [x_blocks(0, 0, 8)],
        [4, 4, 8, 8, 8],
        "sum_cores",
    )
    got_a = shifted(far_a, "seq", 16)
    got_b = shifted(far_b, "seq", -16)
    ahead = jnp.concatenate([add(ahead[:4], got_a), ahead[4:]], axis=0)
    behind = jnp.concatenate([behind[:4], add(behind[4:], got_b)], axis=0)
    got_a = shifted(ahead, "seq", 16)
    got_b = shifted(behind, "seq", -16)
    kept, got = here, got_a.astype(f32) + got_b.astype(f32)
    for bit, count in ((0, 4), (1, 2), (2, 1)):
        kept, away = stage(
            at,
            kept,
            got,
            [z_blocks(bit, count, False), z_blocks(bit, count, True)],
            [count, count],
            f"sum_z{bit}",
        )
        got = swapped(away, 2 << bit)
    return kept[0].astype(f32) + got[0].astype(f32)


def on_device(tokens, cotangent, w_query, w_key, w_value, w_out):
    place = lax.axis_index("seq")
    at = jnp.stack([lax.axis_index("head"), place % 2, place // 16, place // 2 % 8])
    at = at.astype(jnp.int32)
    key_value, own_2, own_4, own_8 = project_kv(tokens, w_key, w_value)
    level_two = swapped(own_4, 1)
    level_three_a = swapped(own_8, 2)
    level_three_b = swapped(own_8, 3)
    queries, d_attended = project_q(tokens, cotangent, w_query, w_out)
    entries = (key_value, own_2, level_two, level_three_a, level_three_b)
    attended_t, stats = attend(entries, queries)
    layer_out = head_sum(*project_out(at, attended_t, w_out))
    query_grad_t, own, grad_2, grad_3 = attend_grads(entries, queries, d_attended, stats)
    got_2 = swapped(grad_2, 1)
    got_3a = swapped(grad_3[: BLOCK // 2], 2)
    got_3b = swapped(grad_3[BLOCK // 2 :], 3)
    *parts, kv_grad = project_input(
        at, own, got_2, got_3a, got_3b, query_grad_t, w_query, w_key, w_value
    )
    grad_tokens = head_sum(*parts)
    mine, other = weight_grads(at, tokens, cotangent, attended_t, query_grad_t, kv_grad)
    scale = 1.0 / math.sqrt(lax.axis_size("seq") * tokens.shape[0])
    summed = seq_sum(at, mine, other) * scale
    return (
        layer_out,
        grad_tokens,
        summed[:16],
        summed[16:32],
        summed[32:48],
        summed[48:].T,
    )


def solution(mesh):
    return jax.shard_map(
        on_device,
        mesh=mesh,
        in_specs=(
            P("seq", None),
            P("seq", None),
            P(None, "head"),
            P(None, "head"),
            P(None, "head"),
            P("head", None),
        ),
        out_specs=(
            P("seq", "head"),
            P("seq", "head"),
            P("seq", "head"),
            P("seq", "head"),
            P("seq", "head"),
            P("head", "seq"),
        ),
        check_vma=False,
    )
```

```python
import functools
import math

import jax
import jax.numpy as jnp
from jax import lax
from jax.experimental import pallas as pl
from jax.experimental.pallas import tpu as pltpu
from jax.sharding import PartitionSpec as P

HEAD_DIM = 64
BLOCK = 256
SPAN = 2 * BLOCK
KEYS = 5 * BLOCK
ROWS = 4 * BLOCK
WIDTH = 1024
COLS = 256
MIB = 1024 * 1024
OFFSETS = (0.0, 0.0, 1.0, 2.0, 3.0)
SCORE_SCALE = 1.0 / (math.log(2.0) * math.sqrt(HEAD_DIM))
INV_ROOT = 1.0 / math.sqrt(HEAD_DIM)
bf16 = jnp.bfloat16
f32 = jnp.float32


def dot_nn(a, b):
    return lax.dot_general(a, b, (((1,), (0,)), ((), ())), preferred_element_type=f32)


def dot_nt(a, b):
    return lax.dot_general(a, b, (((1,), (1,)), ((), ())), preferred_element_type=f32)


def params(mib):
    return pltpu.CompilerParams(vmem_limit_bytes=mib * MIB)


def shape(dims, dtype=bf16):
    return jax.ShapeDtypeStruct(dims, dtype)


def cost(macs, nbytes):
    return pl.CostEstimate(flops=2 * macs, bytes_accessed=nbytes, transcendentals=0)


def run_matrix(rows, cols, shift, expand):
    i = lax.broadcasted_iota(jnp.int32, (rows, cols), 0)
    j = lax.broadcasted_iota(jnp.int32, (rows, cols), 1)
    inside = (i >> shift) == j if expand else i == (j >> shift)
    return jnp.where(inside, 2.0**-shift, 0.0).astype(bf16)


class Copies:
    def __init__(self, sems):
        self.sems = sems
        self.count = 0

    def start(self, source, target):
        copy = pltpu.make_async_copy(source, target, self.sems.at[self.count])
        self.count += 1
        copy.start()
        return copy


def row_block(ref, index, count):
    return ref.at[pl.ds(index * count, count)]


def any_spec():
    return pl.BlockSpec(memory_space=pl.ANY)


def kv_kernel(
    x_hbm, wk_hbm, wv_hbm, kv_hbm, c2_hbm, c4_hbm, c8_hbm,
    x_s, wk_s, wv_s, kv_s, c2_s, c4_s, c8_s, in_sems, out_sems,
):
    fetch, store = Copies(in_sems), Copies(out_sems)
    wk = [fetch.start(row_block(wk_hbm, i, SPAN), row_block(wk_s, i, SPAN)) for i in range(2)]
    x = [fetch.start(row_block(x_hbm, i, BLOCK), row_block(x_s, i, BLOCK)) for i in range(2)]
    wv = [fetch.start(row_block(wv_hbm, i, SPAN), row_block(wv_s, i, SPAN)) for i in range(2)]
    x += [fetch.start(row_block(x_hbm, i, BLOCK), row_block(x_s, i, BLOCK)) for i in (2, 3)]
    averages = [run_matrix(BLOCK >> shift, BLOCK, shift, False) for shift in range(4)]
    stores = []
    for half in range(2):
        if half == 0:
            for copy in wk:
                copy.wait()
        for copy in x[2 * half : 2 * half + 2]:
            copy.wait()
        rows = slice(half * SPAN, (half + 1) * SPAN)
        kv_s[rows, :COLS] = dot_nn(x_s[rows], wk_s[...]).astype(bf16)
        if half == 0:
            for copy in wv:
                copy.wait()
        kv_s[rows, COLS:] = dot_nn(x_s[rows], wv_s[...]).astype(bf16)
        for shift, ref, out in ((3, c8_s, c8_hbm), (2, c4_s, c4_hbm), (1, c2_s, c2_hbm)):
            count = BLOCK >> shift
            for index in (2 * half, 2 * half + 1):
                kv = kv_s[index * BLOCK : (index + 1) * BLOCK]
                mean = dot_nn(averages[shift], kv).astype(bf16)
                ref[index * count : (index + 1) * count] = mean
            stores.append(
                store.start(row_block(ref, half, 2 * count), row_block(out, half, 2 * count))
            )
        stores.append(store.start(row_block(kv_s, half, SPAN), row_block(kv_hbm, half, SPAN)))
    for copy in stores:
        copy.wait()


def project_kv(tokens, w_key, w_value):
    outs = [(ROWS >> s, 2 * COLS) for s in range(4)]
    return pl.pallas_call(
        kv_kernel,
        in_specs=[any_spec()] * 3,
        out_specs=[any_spec()] * 4,
        out_shape=[shape(dims) for dims in outs],
        scratch_shapes=[
            pltpu.VMEM((ROWS, WIDTH), bf16),
            pltpu.VMEM((WIDTH, COLS), bf16),
            pltpu.VMEM((WIDTH, COLS), bf16),
        ]
        + [pltpu.VMEM(dims, bf16) for dims in outs]
        + [pltpu.SemaphoreType.DMA((8,)), pltpu.SemaphoreType.DMA((8,))],
        compiler_params=params(60),
        cost_estimate=cost(ROWS * WIDTH * 2 * COLS, 6 * MIB),
        name="project_kv",
    )(tokens, w_key, w_value)


def q_kernel(
    x_hbm, c_hbm, wq_hbm, wo_hbm, q_hbm, da_hbm,
    x_s, c_s, wq_s, wo_s, q_s, da_s, in_sems, out_sems,
):
    fetch, store = Copies(in_sems), Copies(out_sems)
    wq = [fetch.start(row_block(wq_hbm, i, SPAN), row_block(wq_s, i, SPAN)) for i in range(2)]
    x = [fetch.start(row_block(x_hbm, i, SPAN), row_block(x_s, i, SPAN)) for i in range(2)]
    wo = [fetch.start(row_block(wo_hbm, i, 128), row_block(wo_s, i, 128)) for i in range(2)]
    c = [fetch.start(row_block(c_hbm, i, SPAN), row_block(c_s, i, SPAN)) for i in range(2)]
    stores = []
    for weights, inputs, w_s, in_s, out_s, out, dot in (
        (wq, x, wq_s, x_s, q_s, q_hbm, dot_nn),
        (wo, c, wo_s, c_s, da_s, da_hbm, dot_nt),
    ):
        for copy in weights:
            copy.wait()
        for half in range(2):
            inputs[half].wait()
            rows = slice(half * SPAN, (half + 1) * SPAN)
            out_s[rows] = dot(in_s[rows], w_s[...]).astype(bf16)
            stores.append(store.start(row_block(out_s, half, SPAN), row_block(out, half, SPAN)))
    for copy in stores:
        copy.wait()


def project_q(tokens, cotangent, w_query, w_out):
    return pl.pallas_call(
        q_kernel,
        in_specs=[any_spec()] * 4,
        out_specs=[any_spec()] * 2,
        out_shape=[shape((ROWS, COLS))] * 2,
        scratch_shapes=[
            pltpu.VMEM((ROWS, WIDTH), bf16),
            pltpu.VMEM((ROWS, WIDTH), bf16),
            pltpu.VMEM((WIDTH, COLS), bf16),
            pltpu.VMEM((COLS, WIDTH), bf16),
            pltpu.VMEM((ROWS, COLS), bf16),
            pltpu.VMEM((ROWS, COLS), bf16),
            pltpu.SemaphoreType.DMA((8,)),
            pltpu.SemaphoreType.DMA((4,)),
        ],
        compiler_params=params(60),
        cost_estimate=cost(ROWS * WIDTH * 2 * COLS, 7 * MIB),
        name="project_q",
    )(tokens, cotangent, w_query, w_out)


def entry_rows(refs, kb, lo):
    near, c2, l2, l3a, l3b = refs
    if kb < 2:
        return near[kb * BLOCK : (kb + 1) * BLOCK, lo : lo + 128]
    if kb == 2:
        return c2[:, lo : lo + 128]
    if kb == 3:
        return l2[:, lo : lo + 128]
    return jnp.concatenate([l3a[:, lo : lo + 128], l3b[:, lo : lo + 128]], axis=0)


def only_head(ref, head):
    lane = lax.broadcasted_iota(jnp.int32, (SPAN, 128), 1)
    keep = lane < HEAD_DIM if head % 2 == 0 else lane >= HEAD_DIM
    pair = head // 2 * 128
    return jnp.where(keep, ref[:, pair : pair + 128], jnp.zeros((), bf16))


def fold(values, combine):
    return combine(values.reshape(BLOCK // 8, 8, SPAN), axis=0)


def forward_kernel(*refs):
    entries, q_ref, da_ref, ot_ref, stat_ref = refs[:5], *refs[5:9]
    t_s, vt_s, qm_s, dm_s = refs[9:]
    for kb in range(5):
        rows = slice(kb * BLOCK, (kb + 1) * BLOCK)
        for pair in range(2):
            vt_s[pair * 128 : pair * 128 + 128, rows] = entry_rows(
                entries, kb, COLS + pair * 128
            ).T
    for head in range(4):
        qm_s[head] = only_head(q_ref, head)
        dm_s[head] = only_head(da_ref, head)
    for head in range(4):
        lo = head // 2 * 128
        slot = head % 2
        tops = []
        for kb in range(5):
            rows = slice(kb * BLOCK, (kb + 1) * BLOCK)
            t = dot_nt(entry_rows(entries, kb, lo), qm_s[head]) * SCORE_SCALE
            t_s[slot, rows] = t
            tops.append(fold(t, jnp.max) + OFFSETS[kb])
        top = jnp.max(functools.reduce(jnp.maximum, tops), axis=0, keepdims=True)
        total = jnp.zeros((8, SPAN), f32)
        inner = jnp.zeros((8, SPAN), f32)
        out = jnp.zeros((HEAD_DIM, SPAN), f32)
        mine = slice(head * HEAD_DIM, (head + 1) * HEAD_DIM)
        for kb in range(5):
            rows = slice(kb * BLOCK, (kb + 1) * BLOCK)
            raised = jnp.exp2(t_s[slot, rows] + (OFFSETS[kb] - top))
            p = dot_nt(entry_rows(entries, kb, COLS + lo), dm_s[head])
            total = total + fold(raised, jnp.sum)
            inner = inner + fold(raised * p, jnp.sum)
            out = out + dot_nn(vt_s[mine, rows], raised.astype(bf16))
        total = jnp.sum(total, axis=0, keepdims=True)
        inverse = 1.0 / total
        ot_ref[mine] = (out * inverse).astype(bf16)
        stat_ref[head : head + 1] = top + jnp.log2(total)
        stat_ref[head + 4 : head + 5] = jnp.sum(inner, axis=0, keepdims=True) * inverse


def attend(entries, queries, d_attended):
    part = pl.BlockSpec((SPAN, COLS), lambda i: (i, 0))
    return pl.pallas_call(
        forward_kernel,
        grid=(2,),
        in_specs=[
            pl.BlockSpec((SPAN, 2 * COLS), lambda i: (i, 0)),
            pl.BlockSpec((BLOCK, 2 * COLS), lambda i: (1 - i, 0)),
            pl.BlockSpec((BLOCK, 2 * COLS), lambda i: (0, 0)),
            pl.BlockSpec((BLOCK // 2, 2 * COLS), lambda i: (0, 0)),
            pl.BlockSpec((BLOCK // 2, 2 * COLS), lambda i: (0, 0)),
            part,
            part,
        ],
        out_specs=[
            pl.BlockSpec((COLS, SPAN), lambda i: (0, i)),
            pl.BlockSpec((8, SPAN), lambda i: (0, i)),
        ],
        out_shape=[shape((COLS, ROWS)), shape((8, ROWS), f32)],
        scratch_shapes=[
            pltpu.VMEM((2, KEYS, SPAN), f32),
            pltpu.VMEM((COLS, KEYS), bf16),
            pltpu.VMEM((4, SPAN, 128), bf16),
            pltpu.VMEM((4, SPAN, 128), bf16),
        ],
        compiler_params=params(60),
        cost_estimate=cost(4 * 3 * 4 * ROWS * KEYS * 64, 4 * MIB),
        name="attend",
    )(*entries, queries, d_attended)


def block_grads(key_rows, value_rows, keys_t, offset, qm, dm, stat, inner):
    t = dot_nt(key_rows, qm) * SCORE_SCALE
    attention = jnp.exp2(t + (offset - stat))
    weights = attention.astype(bf16)
    p = dot_nt(value_rows, dm)
    scores = (attention * (p - inner)).astype(bf16)
    return dot_nn(keys_t, scores), dot_nn(scores, qm), dot_nn(weights, dm)


def far_kernel(l2, l3a, l3b, q_ref, da_ref, stat_ref, qgt_ref, g2_ref, g3a_ref, g3b_ref,
               kt_s, qm_s, dm_s, grad_s):
    step = pl.program_id(0)
    refs = (None, None, None, l2, l3a, l3b)

    @pl.when(step == 0)
    def _():
        for kb in (3, 4):
            rows = slice((kb - 3) * BLOCK, (kb - 2) * BLOCK)
            for pair in range(2):
                part = entry_rows(refs[1:], kb, pair * 128)
                kt_s[pair * 128 : pair * 128 + 128, rows] = part.T
        grad_s[...] = jnp.zeros_like(grad_s)

    for head in range(4):
        qm_s[head] = only_head(q_ref, head)
        dm_s[head] = only_head(da_ref, head)
    for pair in range(2):
        lo = pair * 128
        query_grad = [jnp.zeros((HEAD_DIM, SPAN), f32)] * 2
        for kb in (3, 4):
            rows = slice((kb - 3) * BLOCK, (kb - 2) * BLOCK)
            key_grad = value_grad = 0.0
            for side in range(2):
                head = 2 * pair + side
                dq, dk, dv = block_grads(
                    entry_rows(refs[1:], kb, lo),
                    entry_rows(refs[1:], kb, COLS + lo),
                    kt_s[head * HEAD_DIM : (head + 1) * HEAD_DIM, rows],
                    OFFSETS[kb],
                    qm_s[head],
                    dm_s[head],
                    stat_ref[head : head + 1],
                    stat_ref[head + 4 : head + 5],
                )
                query_grad[side] = query_grad[side] + dq
                key_grad, value_grad = key_grad + dk, value_grad + dv
            grad_s[rows, lo : lo + 128] += key_grad
            grad_s[rows, COLS + lo : COLS + lo + 128] += value_grad
        for side in range(2):
            start = (2 * pair + side) * HEAD_DIM
            qgt_ref[start : start + HEAD_DIM] = query_grad[side]

    @pl.when(step == 1)
    def _():
        for ref, first, count in ((g2_ref, 0, 256), (g3a_ref, 256, 128), (g3b_ref, 384, 128)):
            rows = slice(first, first + count)
            ref[:, :COLS] = (grad_s[rows, :COLS] * INV_ROOT).astype(bf16)
            ref[:, COLS:] = grad_s[rows, COLS:].astype(bf16)


def far_grads(level_two, three_a, three_b, queries, d_attended, stats):
    part = pl.BlockSpec((SPAN, COLS), lambda i: (i, 0))
    two = pl.BlockSpec((BLOCK, 2 * COLS), lambda i: (0, 0))
    three = pl.BlockSpec((BLOCK // 2, 2 * COLS), lambda i: (0, 0))
    return pl.pallas_call(
        far_kernel,
        grid=(2,),
        in_specs=[two, three, three, part, part, pl.BlockSpec((8, SPAN), lambda i: (0, i))],
        out_specs=[pl.BlockSpec((COLS, SPAN), lambda i: (0, i)), two, three, three],
        out_shape=[
            shape((COLS, ROWS), f32),
            shape((BLOCK, 2 * COLS)),
            shape((BLOCK // 2, 2 * COLS)),
            shape((BLOCK // 2, 2 * COLS)),
        ],
        scratch_shapes=[
            pltpu.VMEM((COLS, 2 * BLOCK), bf16),
            pltpu.VMEM((4, SPAN, 128), bf16),
            pltpu.VMEM((4, SPAN, 128), bf16),
            pltpu.VMEM((2 * BLOCK, 2 * COLS), f32),
        ],
        compiler_params=params(60),
        cost_estimate=cost(4 * 5 * 4 * ROWS * 2 * BLOCK * 64, 4 * MIB),
        name="far_grads",
    )(level_two, three_a, three_b, queries, d_attended, stats)


def near_kernel(near, c2, q_ref, da_ref, stat_ref, part_ref, qgt_ref, own_ref, sib_ref,
                kt_s, qm_s, dm_s):
    refs = (near, c2, None, None, None)
    for kb in range(3):
        rows = slice(kb * BLOCK, (kb + 1) * BLOCK)
        for pair in range(2):
            part = entry_rows(refs, kb, pair * 128)
            kt_s[pair * 128 : pair * 128 + 128, rows] = part.T
    for head in range(4):
        qm_s[head] = only_head(q_ref, head)
        dm_s[head] = only_head(da_ref, head)
    for pair in range(2):
        lo = pair * 128
        query_grad = []
        for side in range(2):
            start = (2 * pair + side) * HEAD_DIM
            query_grad.append(part_ref[start : start + HEAD_DIM])
        for kb in range(3):
            rows = slice(kb * BLOCK, (kb + 1) * BLOCK)
            key_grad = value_grad = 0.0
            for side in range(2):
                head = 2 * pair + side
                dq, dk, dv = block_grads(
                    entry_rows(refs, kb, lo),
                    entry_rows(refs, kb, COLS + lo),
                    kt_s[head * HEAD_DIM : (head + 1) * HEAD_DIM, rows],
                    OFFSETS[kb],
                    qm_s[head],
                    dm_s[head],
                    stat_ref[head : head + 1],
                    stat_ref[head + 4 : head + 5],
                )
                query_grad[side] = query_grad[side] + dq
                key_grad, value_grad = key_grad + dk, value_grad + dv
            key_grad = key_grad * INV_ROOT
            if kb < 2:
                own_ref[rows, lo : lo + 128] = key_grad
                own_ref[rows, COLS + lo : COLS + lo + 128] = value_grad
            else:
                sib_ref[:, lo : lo + 128] = key_grad
                sib_ref[:, COLS + lo : COLS + lo + 128] = value_grad
        for side in range(2):
            start = (2 * pair + side) * HEAD_DIM
            qgt_ref[start : start + HEAD_DIM] = (query_grad[side] * INV_ROOT).astype(bf16)


def near_grads(key_value, own_2, queries, d_attended, stats, query_part):
    part = pl.BlockSpec((SPAN, COLS), lambda i: (i, 0))
    turned = pl.BlockSpec((COLS, SPAN), lambda i: (0, i))
    near = pl.BlockSpec((SPAN, 2 * COLS), lambda i: (i, 0))
    sibling = pl.BlockSpec((BLOCK, 2 * COLS), lambda i: (1 - i, 0))
    return pl.pallas_call(
        near_kernel,
        grid=(2,),
        in_specs=[near, sibling, part, part, pl.BlockSpec((8, SPAN), lambda i: (0, i)), turned],
        out_specs=[turned, near, sibling],
        out_shape=[
            shape((COLS, ROWS)),
            shape((ROWS, 2 * COLS), f32),
            shape((SPAN, 2 * COLS), f32),
        ],
        scratch_shapes=[
            pltpu.VMEM((COLS, 3 * BLOCK), bf16),
            pltpu.VMEM((4, SPAN, 128), bf16),
            pltpu.VMEM((4, SPAN, 128), bf16),
        ],
        compiler_params=params(60),
        cost_estimate=cost(4 * 5 * 4 * ROWS * 3 * BLOCK * 64, 8 * MIB),
        name="near_grads",
    )(key_value, own_2, queries, d_attended, stats, query_part)


def split_product(matrix, values):
    high = values.astype(bf16)
    low = (values - high.astype(f32)).astype(bf16)
    return dot_nn(matrix, high) + dot_nn(matrix, low)


def out_kernel(ot_ref, w_ref, out_ref):
    out_ref[...] = dot_nn(ot_ref[...].T, w_ref[...]).astype(bf16)


def project_out(attended_t, w_out):
    return pl.pallas_call(
        out_kernel,
        grid=(2,),
        in_specs=[
            pl.BlockSpec((COLS, SPAN), lambda i: (0, i)),
            pl.BlockSpec((COLS, WIDTH), lambda i: (0, 0)),
        ],
        out_specs=pl.BlockSpec((SPAN, WIDTH), lambda i: (i, 0)),
        out_shape=shape((ROWS, WIDTH)),
        compiler_params=params(24),
        cost_estimate=cost(ROWS * WIDTH * COLS, 4 * MIB),
        name="project_out",
    )(attended_t, w_out)


def swapped(value, bits):
    return lax.ppermute(value, "seq", [(i, i ^ bits) for i in range(lax.axis_size("seq"))])


def add(*terms):
    return sum(term.astype(f32) for term in terms).astype(bf16)


def head_sum(part):
    return lax.psum_scatter(part, "head", scatter_dimension=1, tiled=True)


def tail_kernel(
    at_ref, own_hbm, sib_hbm, got2_hbm, got3_hbm, qgt_hbm, ot_hbm, x_hbm, c_hbm,
    wq_hbm, wk_hbm, wv_hbm, part_hbm, mine_hbm, other_hbm,
    own_s, sib_s, got2_s, got3_s, qgt_s, ot_s, x_s, c_s, wq_s, wk_s, wv_s,
    part_s, kvg_s, g_s, in_sems, out_sems,
):
    core = at_ref[0]
    fetch, store = Copies(in_sems), Copies(out_sems)

    def halves(source, target):
        count = source.shape[0] // 2
        return [
            fetch.start(row_block(source, i, count), row_block(target, i, count)) for i in range(2)
        ]

    def wait(*copies):
        for copy in copies:
            copy.wait()

    ot = halves(ot_hbm, ot_s)
    c = halves(c_hbm, c_s)
    qgt = halves(qgt_hbm, qgt_s)
    x = halves(x_hbm, x_s)
    got = halves(got2_hbm, got2_s) + halves(got3_hbm, got3_s)
    sib = halves(sib_hbm, sib_s)
    own = halves(own_hbm, own_s)
    wq, wk, wv = halves(wq_hbm, wq_s), halves(wk_hbm, wk_s), halves(wv_hbm, wv_s)
    stores = []

    def finish(index, grad_t):
        g_s[index] = grad_t.astype(bf16).T.reshape(32, 2, 16, COLS)
        rows = pl.ds(index * 16, 16)
        stores.append(store.start(g_s.at[index, :, 1 - core], other_hbm.at[:, rows]))
        stores.append(store.start(g_s.at[index, :, core], mine_hbm.at[:, rows]))

    wait(*ot, *c)
    finish(0, dot_nn(ot_s[...], c_s[...]))
    wait(*qgt, *x)
    finish(1, dot_nn(qgt_s[...], x_s[...]))
    wait(*got, *sib)
    spread2 = run_matrix(SPAN, SPAN >> 1, 1, True)
    spread4 = run_matrix(SPAN, SPAN >> 2, 2, True)
    spread8 = run_matrix(SPAN, SPAN >> 3, 3, True)
    for half in range(2):
        own[half].wait()
        rows = slice(half * SPAN, (half + 1) * SPAN)
        total = own_s[rows] + split_product(spread2, sib_s[half * 256 : half * 256 + 256])
        total = total + dot_nn(spread4, got2_s[half * 128 : half * 128 + 128])
        total = total + dot_nn(spread8, got3_s[half * 64 : half * 64 + 64])
        kvg_s[rows] = total.astype(bf16)
    for index in range(2):
        finish(2 + index, dot_nn(kvg_s[:, index * COLS : (index + 1) * COLS].T, x_s[...]))
    wait(*wq, *wk, *wv)
    for half in range(2):
        rows = slice(half * SPAN, (half + 1) * SPAN)
        query_grad = qgt_s[:, rows].T
        for start in range(0, WIDTH, COLS):
            cols = slice(start, start + COLS)
            part = dot_nt(query_grad, wq_s[cols, :])
            part = part + dot_nt(kvg_s[rows, :COLS], wk_s[cols, :])
            part = part + dot_nt(kvg_s[rows, COLS:], wv_s[cols, :])
            part_s[rows, cols] = part.astype(bf16)
        stores.append(store.start(row_block(part_s, half, SPAN), row_block(part_hbm, half, SPAN)))
    wait(*stores)


def tail(at, *operands):
    dims = [operand.shape for operand in operands]
    return pl.pallas_call(
        tail_kernel,
        in_specs=[pl.BlockSpec(memory_space=pltpu.SMEM)] + [any_spec()] * len(operands),
        out_specs=[any_spec()] * 3,
        out_shape=[shape((ROWS, WIDTH))] + [shape((32, 64, COLS))] * 2,
        scratch_shapes=[pltpu.VMEM(o.shape, o.dtype) for o in operands]
        + [
            pltpu.VMEM((ROWS, WIDTH), bf16),
            pltpu.VMEM((ROWS, 2 * COLS), bf16),
            pltpu.VMEM((4, 32, 2, 16, COLS), bf16),
            pltpu.SemaphoreType.DMA((2 * len(dims),)),
            pltpu.SemaphoreType.DMA((10,)),
        ],
        compiler_params=params(60),
        cost_estimate=cost(7 * ROWS * WIDTH * COLS, 14 * MIB),
        name="tail",
    )(at, *operands)


def stage_kernel(at_ref, *refs, terms, picks):
    total_s = refs[-1]
    total_s[...] = sum(ref[...].astype(f32) for ref in refs[:terms]).astype(bf16)
    for pick, ref in zip(picks, refs[terms:-1]):
        for block, source in enumerate(pick(at_ref)):
            ref[block] = total_s[source]


def stage(at, terms, picks, counts, name):
    vmem = pl.BlockSpec(memory_space=pltpu.VMEM)
    dims = terms[0].shape
    return pl.pallas_call(
        functools.partial(stage_kernel, terms=len(terms), picks=picks),
        in_specs=[pl.BlockSpec(memory_space=pltpu.SMEM)] + [vmem] * len(terms),
        out_specs=[vmem] * len(counts),
        out_shape=[shape((count, *dims[1:])) for count in counts],
        scratch_shapes=[pltpu.VMEM(dims, bf16)],
        compiler_params=params(24),
        name=name,
    )(at, *terms)


def x_blocks(offset, first, count):
    return lambda at: [((at[1] + offset) & 3) * 8 + first + block for block in range(count)]


def z_blocks(bit, count, flip):
    def pick(at):
        mine = (at[2] >> bit) & 1
        return [2 * block + (1 - mine if flip else mine) for block in range(count)]

    return pick


def moved(value, by):
    size = lax.axis_size("seq")
    return lax.ppermute(value, "seq", [(i, (i + by) % size) for i in range(size)])


def seq_sum(at, mine, other):
    far_a, far_b, ahead, behind, here = stage(
        at,
        (mine, swapped(other, 1)),
        [x_blocks(2, 0, 4), x_blocks(2, 4, 4), x_blocks(1, 0, 8), x_blocks(3, 0, 8)]
        + [x_blocks(0, 0, 8)],
        [4, 4, 8, 8, 8],
        "sum_cores",
    )
    got_a, got_b = moved(far_a, 16), moved(far_b, -16)
    ahead = jnp.concatenate([add(ahead[:4], got_a), ahead[4:]], axis=0)
    behind = jnp.concatenate([behind[:4], add(behind[4:], got_b)], axis=0)
    terms = (here, moved(ahead, 16), moved(behind, -16))
    for bit, count in ((0, 4), (1, 2), (2, 1)):
        kept, away = stage(
            at,
            terms,
            [z_blocks(bit, count, False), z_blocks(bit, count, True)],
            [count, count],
            f"sum_z{bit}",
        )
        terms = (kept, swapped(away, 2 << bit))
    return terms[0][0].astype(f32) + terms[1][0].astype(f32)


def on_device(tokens, cotangent, w_query, w_key, w_value, w_out):
    place = lax.axis_index("seq")
    at = jnp.stack([place % 2, place // 16, place // 2 % 8]).astype(jnp.int32)
    key_value, own_2, own_4, own_8 = project_kv(tokens, w_key, w_value)
    three_a = swapped(own_8, 2)
    level_two = swapped(own_4, 1)
    queries, d_attended = project_q(tokens, cotangent, w_query, w_out)
    queries, three_a = lax.optimization_barrier((queries, three_a))
    three_b = swapped(three_a, 1)
    entries = (key_value, own_2, level_two, three_a, three_b)
    attended_t, stats = attend(entries, queries, d_attended)
    query_part, grad_2, grad_3a, grad_3b = far_grads(
        level_two, three_a, three_b, queries, d_attended, stats
    )
    got_2 = swapped(grad_2, 1)
    got_3b = swapped(grad_3b, 1)
    attended_t, grad_3b = lax.optimization_barrier((attended_t, grad_3b))
    layer_out = head_sum(project_out(attended_t, w_out))
    got_3 = swapped(add(grad_3a, got_3b), 2)
    query_grad_t, own, sibling = near_grads(
        key_value, own_2, queries, d_attended, stats, query_part
    )
    part, mine, other = tail(
        at, own, sibling, got_2, got_3, query_grad_t, attended_t, tokens, cotangent,
        w_query, w_key, w_value,
    )
    grad_tokens = head_sum(part)
    scale = 1.0 / math.sqrt(lax.axis_size("seq") * tokens.shape[0])
    summed = seq_sum(at, mine, other) * scale
    return (
        layer_out,
        grad_tokens,
        summed[16:32],
        summed[32:48],
        summed[48:],
        summed[:16].T,
    )


def solution(mesh):
    return jax.shard_map(
        on_device,
        mesh=mesh,
        in_specs=(
            P("seq", None),
            P("seq", None),
            P(None, "head"),
            P(None, "head"),
            P(None, "head"),
            P("head", None),
        ),
        out_specs=(
            P("seq", "head"),
            P("seq", "head"),
            P("seq", "head"),
            P("seq", "head"),
            P("seq", "head"),
            P("head", "seq"),
        ),
        check_vma=False,
    )
```

```python
import functools
import math

import jax
import jax.numpy as jnp
from jax import lax
from jax.experimental import pallas as pl
from jax.experimental.pallas import tpu as pltpu
from jax.sharding import PartitionSpec as P

HEAD_DIM = 64
BLOCK = 256
SPAN = 2 * BLOCK
KEYS = 5 * BLOCK
ROWS = 4 * BLOCK
WIDTH = 1024
COLS = 256
MIB = 1024 * 1024
OFFSETS = (0.0, 0.0, 1.0, 2.0, 3.0)
SCORE_SCALE = 1.0 / (math.log(2.0) * math.sqrt(HEAD_DIM))
INV_ROOT = 1.0 / math.sqrt(HEAD_DIM)
bf16 = jnp.bfloat16
f32 = jnp.float32


def dot_nn(a, b):
    return lax.dot_general(a, b, (((1,), (0,)), ((), ())), preferred_element_type=f32)


def dot_nt(a, b):
    return lax.dot_general(a, b, (((1,), (1,)), ((), ())), preferred_element_type=f32)


def params(mib):
    return pltpu.CompilerParams(vmem_limit_bytes=mib * MIB)


def shape(dims, dtype=bf16):
    return jax.ShapeDtypeStruct(dims, dtype)


def cost(macs, nbytes):
    return pl.CostEstimate(flops=2 * macs, bytes_accessed=nbytes, transcendentals=0)


def run_matrix(rows, cols, shift, expand):
    i = lax.broadcasted_iota(jnp.int32, (rows, cols), 0)
    j = lax.broadcasted_iota(jnp.int32, (rows, cols), 1)
    inside = (i >> shift) == j if expand else i == (j >> shift)
    return jnp.where(inside, 2.0**-shift, 0.0).astype(bf16)


class Copies:
    def __init__(self, sems):
        self.sems = sems
        self.count = 0

    def start(self, source, target):
        copy = pltpu.make_async_copy(source, target, self.sems.at[self.count])
        self.count += 1
        copy.start()
        return copy


def row_block(ref, index, count):
    return ref.at[pl.ds(index * count, count)]


def any_spec():
    return pl.BlockSpec(memory_space=pl.ANY)


def kv_kernel(
    x_hbm, wk_hbm, wv_hbm, kv_hbm, c2_hbm, c4_hbm, c8_hbm,
    x_s, wk_s, wv_s, kv_s, c2_s, c4_s, c8_s, in_sems, out_sems,
):
    fetch, store = Copies(in_sems), Copies(out_sems)
    wk = [fetch.start(row_block(wk_hbm, i, SPAN), row_block(wk_s, i, SPAN)) for i in range(2)]
    x = [fetch.start(row_block(x_hbm, i, BLOCK), row_block(x_s, i, BLOCK)) for i in range(2)]
    wv = [fetch.start(row_block(wv_hbm, i, SPAN), row_block(wv_s, i, SPAN)) for i in range(2)]
    x += [fetch.start(row_block(x_hbm, i, BLOCK), row_block(x_s, i, BLOCK)) for i in (2, 3)]
    averages = [run_matrix(BLOCK >> shift, BLOCK, shift, False) for shift in range(4)]
    stores = []
    for half in range(2):
        if half == 0:
            for copy in wk:
                copy.wait()
        for copy in x[2 * half : 2 * half + 2]:
            copy.wait()
        rows = slice(half * SPAN, (half + 1) * SPAN)
        kv_s[rows, :COLS] = dot_nn(x_s[rows], wk_s[...]).astype(bf16)
        if half == 0:
            for copy in wv:
                copy.wait()
        kv_s[rows, COLS:] = dot_nn(x_s[rows], wv_s[...]).astype(bf16)
        for shift, ref, out in ((3, c8_s, c8_hbm), (2, c4_s, c4_hbm), (1, c2_s, c2_hbm)):
            count = BLOCK >> shift
            for index in (2 * half, 2 * half + 1):
                kv = kv_s[index * BLOCK : (index + 1) * BLOCK]
                mean = dot_nn(averages[shift], kv).astype(bf16)
                ref[index * count : (index + 1) * count] = mean
            stores.append(
                store.start(row_block(ref, half, 2 * count), row_block(out, half, 2 * count))
            )
        stores.append(store.start(row_block(kv_s, half, SPAN), row_block(kv_hbm, half, SPAN)))
    for copy in stores:
        copy.wait()


def project_kv(tokens, w_key, w_value):
    outs = [(ROWS >> s, 2 * COLS) for s in range(4)]
    return pl.pallas_call(
        kv_kernel,
        in_specs=[any_spec()] * 3,
        out_specs=[any_spec()] * 4,
        out_shape=[shape(dims) for dims in outs],
        scratch_shapes=[
            pltpu.VMEM((ROWS, WIDTH), bf16),
            pltpu.VMEM((WIDTH, COLS), bf16),
            pltpu.VMEM((WIDTH, COLS), bf16),
        ]
        + [pltpu.VMEM(dims, bf16) for dims in outs]
        + [pltpu.SemaphoreType.DMA((8,)), pltpu.SemaphoreType.DMA((8,))],
        compiler_params=params(60),
        cost_estimate=cost(ROWS * WIDTH * 2 * COLS, 6 * MIB),
        name="project_kv",
    )(tokens, w_key, w_value)


def q_kernel(
    x_hbm, c_hbm, wq_hbm, wo_hbm, q_hbm, da_hbm,
    x_s, c_s, wq_s, wo_s, q_s, da_s, in_sems, out_sems,
):
    fetch, store = Copies(in_sems), Copies(out_sems)
    wq = [fetch.start(row_block(wq_hbm, i, SPAN), row_block(wq_s, i, SPAN)) for i in range(2)]
    x = [fetch.start(row_block(x_hbm, i, SPAN), row_block(x_s, i, SPAN)) for i in range(2)]
    wo = [fetch.start(row_block(wo_hbm, i, 128), row_block(wo_s, i, 128)) for i in range(2)]
    c = [fetch.start(row_block(c_hbm, i, SPAN), row_block(c_s, i, SPAN)) for i in range(2)]
    stores = []
    for weights, inputs, w_s, in_s, out_s, out, dot in (
        (wq, x, wq_s, x_s, q_s, q_hbm, dot_nn),
        (wo, c, wo_s, c_s, da_s, da_hbm, dot_nt),
    ):
        for copy in weights:
            copy.wait()
        for half in range(2):
            inputs[half].wait()
            rows = slice(half * SPAN, (half + 1) * SPAN)
            out_s[rows] = dot(in_s[rows], w_s[...]).astype(bf16)
            stores.append(store.start(row_block(out_s, half, SPAN), row_block(out, half, SPAN)))
    for copy in stores:
        copy.wait()


def project_q(tokens, cotangent, w_query, w_out):
    return pl.pallas_call(
        q_kernel,
        in_specs=[any_spec()] * 4,
        out_specs=[any_spec()] * 2,
        out_shape=[shape((ROWS, COLS))] * 2,
        scratch_shapes=[
            pltpu.VMEM((ROWS, WIDTH), bf16),
            pltpu.VMEM((ROWS, WIDTH), bf16),
            pltpu.VMEM((WIDTH, COLS), bf16),
            pltpu.VMEM((COLS, WIDTH), bf16),
            pltpu.VMEM((ROWS, COLS), bf16),
            pltpu.VMEM((ROWS, COLS), bf16),
            pltpu.SemaphoreType.DMA((8,)),
            pltpu.SemaphoreType.DMA((4,)),
        ],
        compiler_params=params(60),
        cost_estimate=cost(ROWS * WIDTH * 2 * COLS, 7 * MIB),
        name="project_q",
    )(tokens, cotangent, w_query, w_out)


def entry_rows(refs, kb, lo):
    near, c2, l2, l3a, l3b = refs
    if kb < 2:
        return near[kb * BLOCK : (kb + 1) * BLOCK, lo : lo + 128]
    if kb == 2:
        return c2[:, lo : lo + 128]
    if kb == 3:
        return l2[:, lo : lo + 128]
    return jnp.concatenate([l3a[:, lo : lo + 128], l3b[:, lo : lo + 128]], axis=0)


def only_head(ref, head):
    lane = lax.broadcasted_iota(jnp.int32, (SPAN, 128), 1)
    keep = lane < HEAD_DIM if head % 2 == 0 else lane >= HEAD_DIM
    pair = head // 2 * 128
    return jnp.where(keep, ref[:, pair : pair + 128], jnp.zeros((), bf16))


def fold(values, combine):
    return combine(values.reshape(BLOCK // 8, 8, SPAN), axis=0)


def forward_kernel(*refs):
    entries, q_ref, da_ref = refs[:5], refs[5], refs[6]
    ot_ref, stat_ref, qgt_ref, g2_ref, g3a_ref, g3b_ref = refs[7:13]
    k_s, v_s, w_s, vt_s, kt_s, qm_s, dm_s, grad_s = refs[13:]
    step = pl.program_id(0)
    for kb in range(5):
        rows = slice(kb * BLOCK, (kb + 1) * BLOCK)
        for pair in range(2):
            lanes = slice(pair * 128, pair * 128 + 128)
            key = entry_rows(entries, kb, pair * 128)
            value = entry_rows(entries, kb, COLS + pair * 128)
            k_s[rows, lanes] = key
            v_s[rows, lanes] = value
            vt_s[lanes, rows] = value.T
            if kb >= 3:
                kt_s[lanes, (kb - 3) * BLOCK : (kb - 2) * BLOCK] = key.T
    for head in range(4):
        qm_s[head] = only_head(q_ref, head)
        dm_s[head] = only_head(da_ref, head)

    @pl.when(step == 0)
    def _():
        grad_s[...] = jnp.zeros_like(grad_s)

    for pair in range(2):
        lo = pair * 128
        key_grad = value_grad = 0.0
        for side in range(2):
            head = 2 * pair + side
            t = dot_nt(k_s[:, lo : lo + 128], qm_s[head])
            p = dot_nt(v_s[:, lo : lo + 128], dm_s[head])
            tops = []
            for kb in range(5):
                rows = slice(kb * BLOCK, (kb + 1) * BLOCK)
                tops.append(fold(t[rows], jnp.max) * SCORE_SCALE + OFFSETS[kb])
            top = jnp.max(functools.reduce(jnp.maximum, tops), axis=0, keepdims=True)
            total = inner = jnp.zeros((8, SPAN), f32)
            far = []
            for kb in range(5):
                rows = slice(kb * BLOCK, (kb + 1) * BLOCK)
                raised = jnp.exp2(t[rows] * SCORE_SCALE + (OFFSETS[kb] - top))
                w_s[side, rows] = raised.astype(bf16)
                total = total + fold(raised, jnp.sum)
                inner = inner + fold(raised * p[rows], jnp.sum)
                if kb >= 3:
                    far.append((raised, p[rows]))
            total = jnp.sum(total, axis=0, keepdims=True)
            inverse = 1.0 / total
            inner = jnp.sum(inner, axis=0, keepdims=True) * inverse
            mine = slice(head * HEAD_DIM, (head + 1) * HEAD_DIM)
            ot_ref[mine] = (dot_nn(vt_s[mine, :], w_s[side]) * inverse).astype(bf16)
            stat_ref[head : head + 1] = top + jnp.log2(total)
            stat_ref[head + 4 : head + 5] = inner
            weights, scores = [], []
            for raised, p_far in far:
                attention = raised * inverse
                weights.append(attention.astype(bf16))
                scores.append((attention * (p_far - inner)).astype(bf16))
            weights, scores = jnp.concatenate(weights, axis=0), jnp.concatenate(scores, axis=0)
            qgt_ref[mine] = dot_nn(kt_s[mine, :], scores)
            key_grad = key_grad + dot_nn(scores, qm_s[head])
            value_grad = value_grad + dot_nn(weights, dm_s[head])
        grad_s[:, lo : lo + 128] += key_grad
        grad_s[:, COLS + lo : COLS + lo + 128] += value_grad

    @pl.when(step == 1)
    def _():
        for ref, first, count in ((g2_ref, 0, 256), (g3a_ref, 256, 128), (g3b_ref, 384, 128)):
            rows = slice(first, first + count)
            ref[:, :COLS] = (grad_s[rows, :COLS] * INV_ROOT).astype(bf16)
            ref[:, COLS:] = grad_s[rows, COLS:].astype(bf16)


def attend(entries, queries, d_attended):
    part = pl.BlockSpec((SPAN, COLS), lambda i: (i, 0))
    turned = pl.BlockSpec((COLS, SPAN), lambda i: (0, i))
    two = pl.BlockSpec((BLOCK, 2 * COLS), lambda i: (0, 0))
    three = pl.BlockSpec((BLOCK // 2, 2 * COLS), lambda i: (0, 0))
    return pl.pallas_call(
        forward_kernel,
        grid=(2,),
        in_specs=[
            pl.BlockSpec((SPAN, 2 * COLS), lambda i: (i, 0)),
            pl.BlockSpec((BLOCK, 2 * COLS), lambda i: (1 - i, 0)),
            two,
            three,
            three,
            part,
            part,
        ],
        out_specs=[turned, pl.BlockSpec((8, SPAN), lambda i: (0, i)), turned, two, three, three],
        out_shape=[
            shape((COLS, ROWS)),
            shape((8, ROWS), f32),
            shape((COLS, ROWS), f32),
            shape((BLOCK, 2 * COLS)),
            shape((BLOCK // 2, 2 * COLS)),
            shape((BLOCK // 2, 2 * COLS)),
        ],
        scratch_shapes=[
            pltpu.VMEM((KEYS, COLS), bf16),
            pltpu.VMEM((KEYS, COLS), bf16),
            pltpu.VMEM((2, KEYS, SPAN), bf16),
            pltpu.VMEM((COLS, KEYS), bf16),
            pltpu.VMEM((COLS, 2 * BLOCK), bf16),
            pltpu.VMEM((4, SPAN, 128), bf16),
            pltpu.VMEM((4, SPAN, 128), bf16),
            pltpu.VMEM((2 * BLOCK, 2 * COLS), f32),
        ],
        compiler_params=params(60),
        cost_estimate=cost(4 * 4 * 4 * ROWS * KEYS * 64, 6 * MIB),
        name="attend",
    )(*entries, queries, d_attended)


def block_grads(key_rows, value_rows, keys_t, offsets, qm, dm, stat, inner):
    t = dot_nt(key_rows, qm) * SCORE_SCALE
    p = dot_nt(value_rows, dm)
    weights, scores = [], []
    for index, offset in enumerate(offsets):
        rows = slice(index * BLOCK, (index + 1) * BLOCK)
        attention = jnp.exp2(t[rows] + (offset - stat))
        weights.append(attention.astype(bf16))
        scores.append((attention * (p[rows] - inner)).astype(bf16))
    weights, scores = jnp.concatenate(weights, axis=0), jnp.concatenate(scores, axis=0)
    return dot_nn(keys_t, scores), dot_nn(scores, qm), dot_nn(weights, dm)


def near_kernel(near, c2, q_ref, da_ref, stat_ref, part_ref, qgt_ref, own_ref, sib_ref,
                kt_s, qm_s, dm_s):
    refs = (near, c2, None, None, None)
    for kb in range(3):
        rows = slice(kb * BLOCK, (kb + 1) * BLOCK)
        for pair in range(2):
            part = entry_rows(refs, kb, pair * 128)
            kt_s[pair * 128 : pair * 128 + 128, rows] = part.T
    for head in range(4):
        qm_s[head] = only_head(q_ref, head)
        dm_s[head] = only_head(da_ref, head)
    for pair in range(2):
        lo = pair * 128
        key_grad = value_grad = 0.0
        stack = [
            jnp.concatenate([entry_rows(refs, kb, first + lo) for kb in range(3)], axis=0)
            for first in (0, COLS)
        ]
        for side in range(2):
            head = 2 * pair + side
            mine = slice(head * HEAD_DIM, (head + 1) * HEAD_DIM)
            dq, dk, dv = block_grads(
                *stack, kt_s[mine, :], OFFSETS[:3], qm_s[head], dm_s[head],
                stat_ref[head : head + 1], stat_ref[head + 4 : head + 5],
            )
            qgt_ref[mine] = ((part_ref[mine] + dq) * INV_ROOT).astype(bf16)
            key_grad, value_grad = key_grad + dk, value_grad + dv
        key_grad = key_grad * INV_ROOT
        own_ref[:, lo : lo + 128] = key_grad[:SPAN]
        own_ref[:, COLS + lo : COLS + lo + 128] = value_grad[:SPAN]
        sib_ref[:, lo : lo + 128] = key_grad[SPAN:]
        sib_ref[:, COLS + lo : COLS + lo + 128] = value_grad[SPAN:]


def near_grads(key_value, own_2, queries, d_attended, stats, query_part):
    part = pl.BlockSpec((SPAN, COLS), lambda i: (i, 0))
    turned = pl.BlockSpec((COLS, SPAN), lambda i: (0, i))
    near = pl.BlockSpec((SPAN, 2 * COLS), lambda i: (i, 0))
    sibling = pl.BlockSpec((BLOCK, 2 * COLS), lambda i: (1 - i, 0))
    return pl.pallas_call(
        near_kernel,
        grid=(2,),
        in_specs=[near, sibling, part, part, pl.BlockSpec((8, SPAN), lambda i: (0, i)), turned],
        out_specs=[turned, near, sibling],
        out_shape=[
            shape((COLS, ROWS)),
            shape((ROWS, 2 * COLS), f32),
            shape((SPAN, 2 * COLS), f32),
        ],
        scratch_shapes=[
            pltpu.VMEM((COLS, 3 * BLOCK), bf16),
            pltpu.VMEM((4, SPAN, 128), bf16),
            pltpu.VMEM((4, SPAN, 128), bf16),
        ],
        compiler_params=params(60),
        cost_estimate=cost(4 * 5 * 4 * ROWS * 3 * BLOCK * 64, 8 * MIB),
        name="near_grads",
    )(key_value, own_2, queries, d_attended, stats, query_part)


def split_product(matrix, values):
    high = values.astype(bf16)
    low = (values - high.astype(f32)).astype(bf16)
    return dot_nn(matrix, high) + dot_nn(matrix, low)


def ring_columns(half):
    return (2, 3, 1, 0) if half == 0 else (1, 2, 3, 0)


def column_group(here, offset):
    return pl.ds(pl.multiple_of(((here + offset) & 3) * COLS, COLS), COLS)


def out_kernel(at_ref, ot_ref, w_ref, right_ref, left_ref, hold_ref, mine_ref):
    outs = (right_ref, left_ref, hold_ref, mine_ref)
    for half in range(2):
        rows = slice(half * SPAN, (half + 1) * SPAN)
        attended = ot_ref[:, rows].T
        for offset, ref in zip(ring_columns(half), outs):
            part = dot_nn(attended, w_ref[:, column_group(at_ref[1], offset)])
            ref[rows] = part.astype(bf16)


def project_out(at, attended_t, w_out):
    vmem = pl.BlockSpec(memory_space=pltpu.VMEM)
    return pl.pallas_call(
        out_kernel,
        in_specs=[pl.BlockSpec(memory_space=pltpu.SMEM), vmem, vmem],
        out_specs=[vmem] * 4,
        out_shape=[shape((ROWS, COLS))] * 4,
        compiler_params=params(24),
        cost_estimate=cost(ROWS * WIDTH * COLS, 4 * MIB),
        name="project_out",
    )(at, attended_t, w_out)


def shifted(value, by):
    size = lax.axis_size("head")
    return lax.ppermute(value, "head", [(i, (i + by) % size) for i in range(size)])


def swapped(value, bits):
    return lax.ppermute(value, "seq", [(i, i ^ bits) for i in range(lax.axis_size("seq"))])


def add(*terms):
    return sum(term.astype(f32) for term in terms).astype(bf16)


def head_sum_first(right, left, hold, mine):
    return shifted(right, 1), shifted(left, -1)


def head_sum_second(got_right, got_left, right, left, hold, mine):
    half = ROWS // 2
    more_right = shifted(add(hold[:half], got_right[:half]), 1)
    more_left = shifted(add(hold[half:], got_left[half:]), -1)
    return more_right, more_left


def head_sum_last(more_right, more_left, got_right, got_left, right, left, hold, mine):
    half = ROWS // 2
    return jnp.concatenate(
        [
            add(mine[:half], got_left[:half], more_right),
            add(mine[half:], got_right[half:], more_left),
        ],
        axis=0,
    )


def head_sum(*parts):
    got = head_sum_first(*parts)
    more = head_sum_second(*got, *parts)
    return head_sum_last(*more, *got, *parts)


def tail_kernel(
    at_ref, own_hbm, sib_hbm, got2_hbm, got3_hbm, qgt_hbm, ot_hbm, x_hbm, c_hbm,
    wq_hbm, wk_hbm, wv_hbm, right_hbm, left_hbm, hold_hbm, stay_hbm, mine_hbm, other_hbm,
    own_s, sib_s, got2_s, got3_s, qgt_s, ot_s, x_s, c_s, wq_s, wk_s, wv_s,
    part_s, kvg_s, g_s, in_sems, out_sems,
):
    core = at_ref[0]
    fetch, store = Copies(in_sems), Copies(out_sems)

    def halves(source, target):
        count = source.shape[0] // 2
        return [
            fetch.start(row_block(source, i, count), row_block(target, i, count)) for i in range(2)
        ]

    def wait(*copies):
        for copy in copies:
            copy.wait()

    ot = halves(ot_hbm, ot_s)
    c = halves(c_hbm, c_s)
    qgt = halves(qgt_hbm, qgt_s)
    x = halves(x_hbm, x_s)
    got = halves(got2_hbm, got2_s) + halves(got3_hbm, got3_s)
    sib = halves(sib_hbm, sib_s)
    own = halves(own_hbm, own_s)
    wq, wk, wv = halves(wq_hbm, wq_s), halves(wk_hbm, wk_s), halves(wv_hbm, wv_s)
    stores = []

    def finish(index, grad_t):
        g_s[index] = grad_t.astype(bf16).T.reshape(32, 2, 16, COLS)
        rows = pl.ds(index * 16, 16)
        stores.append(store.start(g_s.at[index, :, 1 - core], other_hbm.at[:, rows]))
        stores.append(store.start(g_s.at[index, :, core], mine_hbm.at[:, rows]))

    wait(*ot, *c)
    finish(0, dot_nn(ot_s[...], c_s[...]))
    wait(*qgt, *x)
    finish(1, dot_nn(qgt_s[...], x_s[...]))
    wait(*got, *sib)
    spread2 = run_matrix(SPAN, SPAN >> 1, 1, True)
    spread4 = run_matrix(SPAN, SPAN >> 2, 2, True)
    spread8 = run_matrix(SPAN, SPAN >> 3, 3, True)
    for half in range(2):
        own[half].wait()
        rows = slice(half * SPAN, (half + 1) * SPAN)
        total = own_s[rows] + split_product(spread2, sib_s[half * 256 : half * 256 + 256])
        total = total + dot_nn(spread4, got2_s[half * 128 : half * 128 + 128])
        total = total + dot_nn(spread8, got3_s[half * 64 : half * 64 + 64])
        kvg_s[rows] = total.astype(bf16)
    for index in range(2):
        finish(2 + index, dot_nn(kvg_s[:, index * COLS : (index + 1) * COLS].T, x_s[...]))
    wait(*wq, *wk, *wv)
    outs = (right_hbm, left_hbm, hold_hbm, stay_hbm)
    for half in range(2):
        rows = slice(half * SPAN, (half + 1) * SPAN)
        query_grad = qgt_s[:, rows].T
        for index, (offset, out) in enumerate(zip(ring_columns(half), outs)):
            cols = column_group(at_ref[1], offset)
            part = dot_nt(query_grad, wq_s[cols, :])
            part = part + dot_nt(kvg_s[rows, :COLS], wk_s[cols, :])
            part = part + dot_nt(kvg_s[rows, COLS:], wv_s[cols, :])
            part_s[index, rows] = part.astype(bf16)
            stores.append(
                store.start(part_s.at[index, pl.ds(half * SPAN, SPAN)], row_block(out, half, SPAN))
            )
    wait(*stores)


def tail(at, *operands):
    dims = [operand.shape for operand in operands]
    return pl.pallas_call(
        tail_kernel,
        in_specs=[pl.BlockSpec(memory_space=pltpu.SMEM)] + [any_spec()] * len(operands),
        out_specs=[any_spec()] * 6,
        out_shape=[shape((ROWS, COLS))] * 4 + [shape((32, 64, COLS))] * 2,
        scratch_shapes=[pltpu.VMEM(o.shape, o.dtype) for o in operands]
        + [
            pltpu.VMEM((4, ROWS, COLS), bf16),
            pltpu.VMEM((ROWS, 2 * COLS), bf16),
            pltpu.VMEM((4, 32, 2, 16, COLS), bf16),
            pltpu.SemaphoreType.DMA((2 * len(dims),)),
            pltpu.SemaphoreType.DMA((16,)),
        ],
        compiler_params=params(60),
        cost_estimate=cost(7 * ROWS * WIDTH * COLS, 14 * MIB),
        name="tail",
    )(at, *operands)


def seq_sum(mine, got):
    size = lax.axis_size("seq")
    along_x = [list(range(first, size, 16)) for first in range(16)]
    along_z = [list(range(16 * x + core, 16 * x + 16, 2)) for x in range(4) for core in range(2)]
    blocks = add(mine, got).reshape(4, 8, 64, COLS)
    blocks = lax.all_to_all(blocks, "seq", 0, 0, axis_index_groups=along_x)
    blocks = jnp.sum(blocks.astype(f32), axis=0).astype(bf16)
    blocks = lax.all_to_all(blocks, "seq", 0, 0, axis_index_groups=along_z)
    return jnp.sum(blocks.astype(f32), axis=0)


def on_device(tokens, cotangent, w_query, w_key, w_value, w_out):
    at = jnp.stack([lax.axis_index("seq") % 2, lax.axis_index("head")]).astype(jnp.int32)
    key_value, own_2, own_4, own_8 = project_kv(tokens, w_key, w_value)
    three_a = swapped(own_8, 2)
    level_two = swapped(own_4, 1)
    queries, d_attended = project_q(tokens, cotangent, w_query, w_out)
    queries, three_a = lax.optimization_barrier((queries, three_a))
    three_b = swapped(three_a, 1)
    entries = (key_value, own_2, level_two, three_a, three_b)
    attended_t, stats, query_part, grad_2, grad_3a, grad_3b = attend(
        entries, queries, d_attended
    )
    got_2 = swapped(grad_2, 1)
    got_3b = swapped(grad_3b, 1)
    out_parts = project_out(at, attended_t, w_out)
    out_got = head_sum_first(*out_parts)
    grad_3 = add(grad_3a, got_3b)
    near = (key_value, own_2, queries, d_attended, stats, query_part)
    near, out_parts, grad_3 = lax.optimization_barrier((near, out_parts, grad_3))
    got_3 = swapped(grad_3, 2)
    near = near_grads(*near)
    near, out_got = lax.optimization_barrier((near, out_got))
    out_more = head_sum_second(*out_got, *out_parts)
    query_grad_t, own, sibling = near
    *parts, mine, other = tail(
        at, own, sibling, got_2, got_3, query_grad_t, attended_t, tokens, cotangent,
        w_query, w_key, w_value,
    )
    (parts, mine, other), out_more = lax.optimization_barrier(((parts, mine, other), out_more))
    layer_out = head_sum_last(*out_more, *out_got, *out_parts)
    grad_tokens = head_sum(*parts)
    scale = 1.0 / math.sqrt(lax.axis_size("seq") * tokens.shape[0])
    summed = seq_sum(mine, swapped(other, 1)) * scale
    return (
        layer_out,
        grad_tokens,
        summed[16:32],
        summed[32:48],
        summed[48:],
        summed[:16].T,
    )


def solution(mesh):
    return jax.shard_map(
        on_device,
        mesh=mesh,
        in_specs=(
            P("seq", None),
            P("seq", None),
            P(None, "head"),
            P(None, "head"),
            P(None, "head"),
            P("head", None),
        ),
        out_specs=(
            P("seq", "head"),
            P("seq", "head"),
            P("seq", "head"),
            P("seq", "head"),
            P("seq", "head"),
            P("head", "seq"),
        ),
        check_vma=False,
    )
```

```python
import functools
import math

import jax
import jax.numpy as jnp
from jax import lax
from jax.experimental import pallas as pl
from jax.experimental.pallas import tpu as pltpu
from jax.sharding import PartitionSpec as P

HEAD_DIM = 64
BLOCK = 256
SPAN = 2 * BLOCK
KEYS = 5 * BLOCK
ROWS = 4 * BLOCK
WIDTH = 1024
COLS = 256
MIB = 1024 * 1024
OFFSETS = (0.0, 0.0, 1.0, 2.0, 3.0)
SCORE_SCALE = 1.0 / (math.log(2.0) * math.sqrt(HEAD_DIM))
INV_ROOT = 1.0 / math.sqrt(HEAD_DIM)
bf16 = jnp.bfloat16
f32 = jnp.float32


def dot_nn(a, b):
    return lax.dot_general(a, b, (((1,), (0,)), ((), ())), preferred_element_type=f32)


def dot_nt(a, b):
    return lax.dot_general(a, b, (((1,), (1,)), ((), ())), preferred_element_type=f32)


def params(mib):
    return pltpu.CompilerParams(vmem_limit_bytes=mib * MIB)


def shape(dims, dtype=bf16):
    return jax.ShapeDtypeStruct(dims, dtype)


def cost(macs, nbytes):
    return pl.CostEstimate(flops=2 * macs, bytes_accessed=nbytes, transcendentals=0)


def run_matrix(rows, cols, shift, expand):
    i = lax.broadcasted_iota(jnp.int32, (rows, cols), 0)
    j = lax.broadcasted_iota(jnp.int32, (rows, cols), 1)
    inside = (i >> shift) == j if expand else i == (j >> shift)
    return jnp.where(inside, 2.0**-shift, 0.0).astype(bf16)


class Copies:
    def __init__(self, sems):
        self.sems = sems
        self.count = 0

    def start(self, source, target):
        copy = pltpu.make_async_copy(source, target, self.sems.at[self.count])
        self.count += 1
        copy.start()
        return copy


def row_block(ref, index, count):
    return ref.at[pl.ds(index * count, count)]


def any_spec():
    return pl.BlockSpec(memory_space=pl.ANY)


def tokens_kernel(
    x_hbm, wk_hbm, wv_hbm, wq_hbm, kv_hbm, c2_hbm, c4_hbm, c8_hbm, q_hbm,
    x_s, wk_s, wv_s, wq_s, kv_s, c2_s, c4_s, c8_s, q_s, in_sems, out_sems,
):
    fetch, store = Copies(in_sems), Copies(out_sems)
    wk = [fetch.start(row_block(wk_hbm, i, SPAN), row_block(wk_s, i, SPAN)) for i in range(2)]
    x = [fetch.start(row_block(x_hbm, i, BLOCK), row_block(x_s, i, BLOCK)) for i in range(2)]
    wv = [fetch.start(row_block(wv_hbm, i, SPAN), row_block(wv_s, i, SPAN)) for i in range(2)]
    x += [fetch.start(row_block(x_hbm, i, BLOCK), row_block(x_s, i, BLOCK)) for i in (2, 3)]
    wq = [fetch.start(row_block(wq_hbm, i, SPAN), row_block(wq_s, i, SPAN)) for i in range(2)]
    averages = [run_matrix(BLOCK >> shift, BLOCK, shift, False) for shift in range(4)]
    stores = []
    for half in range(2):
        if half == 0:
            for copy in wk:
                copy.wait()
        for copy in x[2 * half : 2 * half + 2]:
            copy.wait()
        rows = slice(half * SPAN, (half + 1) * SPAN)
        kv_s[rows, :COLS] = dot_nn(x_s[rows], wk_s[...]).astype(bf16)
        if half == 0:
            for copy in wv:
                copy.wait()
        kv_s[rows, COLS:] = dot_nn(x_s[rows], wv_s[...]).astype(bf16)
        stores.append(store.start(row_block(kv_s, half, SPAN), row_block(kv_hbm, half, SPAN)))
        for shift, ref, out in ((3, c8_s, c8_hbm), (2, c4_s, c4_hbm), (1, c2_s, c2_hbm)):
            count = BLOCK >> shift
            for index in (2 * half, 2 * half + 1):
                kv = kv_s[index * BLOCK : (index + 1) * BLOCK]
                mean = dot_nn(averages[shift], kv).astype(bf16)
                ref[index * count : (index + 1) * count] = mean
            stores.append(
                store.start(row_block(ref, half, 2 * count), row_block(out, half, 2 * count))
            )
    for copy in wq:
        copy.wait()
    for half in range(2):
        rows = slice(half * SPAN, (half + 1) * SPAN)
        q_s[rows] = dot_nn(x_s[rows], wq_s[...]).astype(bf16)
        stores.append(store.start(row_block(q_s, half, SPAN), row_block(q_hbm, half, SPAN)))
    for copy in stores:
        copy.wait()


def project_tokens(tokens, w_key, w_value, w_query):
    outs = [(ROWS >> s, 2 * COLS) for s in range(4)] + [(ROWS, COLS)]
    return pl.pallas_call(
        tokens_kernel,
        in_specs=[any_spec()] * 4,
        out_specs=[any_spec()] * 5,
        out_shape=[shape(dims) for dims in outs],
        scratch_shapes=[pltpu.VMEM((ROWS, WIDTH), bf16)]
        + [pltpu.VMEM((WIDTH, COLS), bf16)] * 3
        + [pltpu.VMEM(dims, bf16) for dims in outs]
        + [pltpu.SemaphoreType.DMA((10,)), pltpu.SemaphoreType.DMA((10,))],
        compiler_params=params(60),
        cost_estimate=cost(ROWS * WIDTH * 3 * COLS, 7 * MIB),
        name="project_tokens",
    )(tokens, w_key, w_value, w_query)


def cotangent_kernel(c_hbm, wo_hbm, da_hbm, c_s, wo_s, da_s, in_sems, out_sems):
    fetch, store = Copies(in_sems), Copies(out_sems)
    wo = [fetch.start(row_block(wo_hbm, i, 128), row_block(wo_s, i, 128)) for i in range(2)]
    c = [fetch.start(row_block(c_hbm, i, BLOCK), row_block(c_s, i, BLOCK)) for i in range(4)]
    for copy in wo:
        copy.wait()
    stores = []
    for half in range(2):
        for copy in c[2 * half : 2 * half + 2]:
            copy.wait()
        rows = slice(half * SPAN, (half + 1) * SPAN)
        da_s[rows] = dot_nt(c_s[rows], wo_s[...]).astype(bf16)
        stores.append(store.start(row_block(da_s, half, SPAN), row_block(da_hbm, half, SPAN)))
    for copy in stores:
        copy.wait()


def project_cotangent(cotangent, w_out):
    return pl.pallas_call(
        cotangent_kernel,
        in_specs=[any_spec()] * 2,
        out_specs=any_spec(),
        out_shape=shape((ROWS, COLS)),
        scratch_shapes=[
            pltpu.VMEM((ROWS, WIDTH), bf16),
            pltpu.VMEM((COLS, WIDTH), bf16),
            pltpu.VMEM((ROWS, COLS), bf16),
            pltpu.SemaphoreType.DMA((6,)),
            pltpu.SemaphoreType.DMA((2,)),
        ],
        compiler_params=params(60),
        cost_estimate=cost(ROWS * WIDTH * COLS, 4 * MIB),
        name="project_cotangent",
    )(cotangent, w_out)


def entry_rows(refs, kb, lo):
    near, c2, l2, l3a, l3b = refs
    if kb < 2:
        return near[kb * BLOCK : (kb + 1) * BLOCK, lo : lo + 128]
    if kb == 2:
        return c2[:, lo : lo + 128]
    if kb == 3:
        return l2[:, lo : lo + 128]
    return jnp.concatenate([l3a[:, lo : lo + 128], l3b[:, lo : lo + 128]], axis=0)


def only_head(ref, head):
    lane = lax.broadcasted_iota(jnp.int32, (SPAN, 128), 1)
    keep = lane < HEAD_DIM if head % 2 == 0 else lane >= HEAD_DIM
    pair = head // 2 * 128
    return jnp.where(keep, ref[:, pair : pair + 128], jnp.zeros((), bf16))


def fold(values, combine):
    return combine(values.reshape(BLOCK // 8, 8, SPAN), axis=0)


def forward_kernel(*refs):
    entries, q_ref, da_ref = refs[:5], refs[5], refs[6]
    ot_ref, stat_ref, qgt_ref, g2_ref, g3a_ref, g3b_ref = refs[7:13]
    w_s, vt_s, kt_s, qm_s, dm_s, grad_s = refs[13:]
    step = pl.program_id(0)
    for kb in range(5):
        rows = slice(kb * BLOCK, (kb + 1) * BLOCK)
        for pair in range(2):
            lanes = slice(pair * 128, pair * 128 + 128)
            vt_s[lanes, rows] = entry_rows(entries, kb, COLS + pair * 128).T
            if kb >= 3:
                key = entry_rows(entries, kb, pair * 128)
                kt_s[lanes, (kb - 3) * BLOCK : (kb - 2) * BLOCK] = key.T
    for head in range(4):
        qm_s[head] = only_head(q_ref, head)
        dm_s[head] = only_head(da_ref, head)

    @pl.when(step == 0)
    def _():
        grad_s[...] = jnp.zeros_like(grad_s)

    for pair in range(2):
        lo = pair * 128
        key_grad = value_grad = 0.0
        keys, values = [
            jnp.concatenate([entry_rows(entries, kb, first + lo) for kb in range(5)], axis=0)
            for first in (0, COLS)
        ]
        for side in range(2):
            head = 2 * pair + side
            t = dot_nt(keys, qm_s[head])
            p = dot_nt(values, dm_s[head])
            tops = []
            for kb in range(5):
                rows = slice(kb * BLOCK, (kb + 1) * BLOCK)
                tops.append(fold(t[rows], jnp.max) * SCORE_SCALE + OFFSETS[kb])
            top = jnp.max(functools.reduce(jnp.maximum, tops), axis=0, keepdims=True)
            total = inner = jnp.zeros((8, SPAN), f32)
            far = []
            for kb in range(5):
                rows = slice(kb * BLOCK, (kb + 1) * BLOCK)
                raised = jnp.exp2(t[rows] * SCORE_SCALE + (OFFSETS[kb] - top))
                w_s[side, rows] = raised.astype(bf16)
                total = total + fold(raised, jnp.sum)
                inner = inner + fold(raised * p[rows], jnp.sum)
                if kb >= 3:
                    far.append((raised, p[rows]))
            total = jnp.sum(total, axis=0, keepdims=True)
            inverse = 1.0 / total
            inner = jnp.sum(inner, axis=0, keepdims=True) * inverse
            mine = slice(head * HEAD_DIM, (head + 1) * HEAD_DIM)
            ot_ref[mine] = (dot_nn(vt_s[mine, :], w_s[side]) * inverse).astype(bf16)
            stat_ref[head : head + 1] = top + jnp.log2(total)
            stat_ref[head + 4 : head + 5] = inner
            weights, scores = [], []
            for raised, p_far in far:
                attention = raised * inverse
                weights.append(attention.astype(bf16))
                scores.append((attention * (p_far - inner)).astype(bf16))
            weights, scores = jnp.concatenate(weights, axis=0), jnp.concatenate(scores, axis=0)
            qgt_ref[mine] = dot_nn(kt_s[mine, :], scores)
            key_grad = key_grad + dot_nn(scores, qm_s[head])
            value_grad = value_grad + dot_nn(weights, dm_s[head])
        grad_s[:, lo : lo + 128] += key_grad
        grad_s[:, COLS + lo : COLS + lo + 128] += value_grad

    @pl.when(step == 1)
    def _():
        for ref, first, count in ((g2_ref, 0, 256), (g3a_ref, 256, 128), (g3b_ref, 384, 128)):
            rows = slice(first, first + count)
            ref[:, :COLS] = (grad_s[rows, :COLS] * INV_ROOT).astype(bf16)
            ref[:, COLS:] = grad_s[rows, COLS:].astype(bf16)


def attend(entries, queries, d_attended):
    part = pl.BlockSpec((SPAN, COLS), lambda i: (i, 0))
    turned = pl.BlockSpec((COLS, SPAN), lambda i: (0, i))
    two = pl.BlockSpec((BLOCK, 2 * COLS), lambda i: (0, 0))
    three = pl.BlockSpec((BLOCK // 2, 2 * COLS), lambda i: (0, 0))
    return pl.pallas_call(
        forward_kernel,
        grid=(2,),
        in_specs=[
            pl.BlockSpec((SPAN, 2 * COLS), lambda i: (i, 0)),
            pl.BlockSpec((BLOCK, 2 * COLS), lambda i: (1 - i, 0)),
            two,
            three,
            three,
            part,
            part,
        ],
        out_specs=[turned, pl.BlockSpec((8, SPAN), lambda i: (0, i)), turned, two, three, three],
        out_shape=[
            shape((COLS, ROWS)),
            shape((8, ROWS), f32),
            shape((COLS, ROWS), f32),
            shape((BLOCK, 2 * COLS)),
            shape((BLOCK // 2, 2 * COLS)),
            shape((BLOCK // 2, 2 * COLS)),
        ],
        scratch_shapes=[
            pltpu.VMEM((2, KEYS, SPAN), bf16),
            pltpu.VMEM((COLS, KEYS), bf16),
            pltpu.VMEM((COLS, 2 * BLOCK), bf16),
            pltpu.VMEM((4, SPAN, 128), bf16),
            pltpu.VMEM((4, SPAN, 128), bf16),
            pltpu.VMEM((2 * BLOCK, 2 * COLS), f32),
        ],
        compiler_params=params(60),
        cost_estimate=cost(4 * 4 * 4 * ROWS * KEYS * 64, 6 * MIB),
        name="attend",
    )(*entries, queries, d_attended)


def block_grads(key_rows, value_rows, keys_t, offsets, qm, dm, stat, inner):
    t = dot_nt(key_rows, qm) * SCORE_SCALE
    p = dot_nt(value_rows, dm)
    weights, scores = [], []
    for index, offset in enumerate(offsets):
        rows = slice(index * BLOCK, (index + 1) * BLOCK)
        attention = jnp.exp2(t[rows] + (offset - stat))
        weights.append(attention.astype(bf16))
        scores.append((attention * (p[rows] - inner)).astype(bf16))
    weights, scores = jnp.concatenate(weights, axis=0), jnp.concatenate(scores, axis=0)
    return dot_nn(keys_t, scores), dot_nn(scores, qm), dot_nn(weights, dm)


def near_kernel(near, c2, q_ref, da_ref, stat_ref, part_ref, qgt_ref, own_ref, sib_ref,
                kt_s, qm_s, dm_s):
    refs = (near, c2, None, None, None)
    for kb in range(3):
        rows = slice(kb * BLOCK, (kb + 1) * BLOCK)
        for pair in range(2):
            part = entry_rows(refs, kb, pair * 128)
            kt_s[pair * 128 : pair * 128 + 128, rows] = part.T
    for head in range(4):
        qm_s[head] = only_head(q_ref, head)
        dm_s[head] = only_head(da_ref, head)
    for pair in range(2):
        lo = pair * 128
        key_grad = value_grad = 0.0
        stack = [
            jnp.concatenate([entry_rows(refs, kb, first + lo) for kb in range(3)], axis=0)
            for first in (0, COLS)
        ]
        for side in range(2):
            head = 2 * pair + side
            mine = slice(head * HEAD_DIM, (head + 1) * HEAD_DIM)
            dq, dk, dv = block_grads(
                *stack, kt_s[mine, :], OFFSETS[:3], qm_s[head], dm_s[head],
                stat_ref[head : head + 1], stat_ref[head + 4 : head + 5],
            )
            qgt_ref[mine] = ((part_ref[mine] + dq) * INV_ROOT).astype(bf16)
            key_grad, value_grad = key_grad + dk, value_grad + dv
        key_grad = key_grad * INV_ROOT
        own_ref[:, lo : lo + 128] = key_grad[:SPAN]
        own_ref[:, COLS + lo : COLS + lo + 128] = value_grad[:SPAN]
        sib_ref[:, lo : lo + 128] = key_grad[SPAN:]
        sib_ref[:, COLS + lo : COLS + lo + 128] = value_grad[SPAN:]


def near_grads(key_value, own_2, queries, d_attended, stats, query_part):
    part = pl.BlockSpec((SPAN, COLS), lambda i: (i, 0))
    turned = pl.BlockSpec((COLS, SPAN), lambda i: (0, i))
    near = pl.BlockSpec((SPAN, 2 * COLS), lambda i: (i, 0))
    sibling = pl.BlockSpec((BLOCK, 2 * COLS), lambda i: (1 - i, 0))
    return pl.pallas_call(
        near_kernel,
        grid=(2,),
        in_specs=[near, sibling, part, part, pl.BlockSpec((8, SPAN), lambda i: (0, i)), turned],
        out_specs=[turned, near, sibling],
        out_shape=[
            shape((COLS, ROWS)),
            shape((ROWS, 2 * COLS), f32),
            shape((SPAN, 2 * COLS), f32),
        ],
        scratch_shapes=[
            pltpu.VMEM((COLS, 3 * BLOCK), bf16),
            pltpu.VMEM((4, SPAN, 128), bf16),
            pltpu.VMEM((4, SPAN, 128), bf16),
        ],
        compiler_params=params(60),
        cost_estimate=cost(4 * 5 * 4 * ROWS * 3 * BLOCK * 64, 8 * MIB),
        name="near_grads",
    )(key_value, own_2, queries, d_attended, stats, query_part)


def split_product(matrix, values):
    high = values.astype(bf16)
    low = (values - high.astype(f32)).astype(bf16)
    return dot_nn(matrix, high) + dot_nn(matrix, low)


def ring_columns(half):
    return (2, 3, 1, 0) if half == 0 else (1, 2, 3, 0)


def column_group(here, offset):
    return pl.ds(pl.multiple_of(((here + offset) & 3) * COLS, COLS), COLS)


def out_kernel(at_ref, ot_ref, w_ref, right_ref, left_ref, hold_ref, mine_ref):
    outs = (right_ref, left_ref, hold_ref, mine_ref)
    for half in range(2):
        rows = slice(half * SPAN, (half + 1) * SPAN)
        attended = ot_ref[:, rows].T
        for offset, ref in zip(ring_columns(half), outs):
            part = dot_nn(attended, w_ref[:, column_group(at_ref[1], offset)])
            ref[rows] = part.astype(bf16)


def project_out(at, attended_t, w_out):
    vmem = pl.BlockSpec(memory_space=pltpu.VMEM)
    return pl.pallas_call(
        out_kernel,
        in_specs=[pl.BlockSpec(memory_space=pltpu.SMEM), vmem, vmem],
        out_specs=[vmem] * 4,
        out_shape=[shape((ROWS, COLS))] * 4,
        compiler_params=params(24),
        cost_estimate=cost(ROWS * WIDTH * COLS, 4 * MIB),
        name="project_out",
    )(at, attended_t, w_out)


def shifted(value, by):
    size = lax.axis_size("head")
    return lax.ppermute(value, "head", [(i, (i + by) % size) for i in range(size)])


def swapped(value, bits):
    return lax.ppermute(value, "seq", [(i, i ^ bits) for i in range(lax.axis_size("seq"))])


def add(*terms):
    return sum(term.astype(f32) for term in terms).astype(bf16)


def head_sum_first(right, left, hold, mine):
    return shifted(right, 1), shifted(left, -1)


def head_sum_second(got_right, got_left, right, left, hold, mine):
    half = ROWS // 2
    return add(hold[:half], got_right[:half]), add(hold[half:], got_left[half:])


def head_sum_third(more_right, more_left):
    return shifted(more_right, 1), shifted(more_left, -1)


def head_sum_last(more_right, more_left, got_right, got_left, right, left, hold, mine):
    half = ROWS // 2
    return jnp.concatenate(
        [
            add(mine[:half], got_left[:half], more_right),
            add(mine[half:], got_right[half:], more_left),
        ],
        axis=0,
    )


def tail_kernel(
    at_ref, own_hbm, sib_hbm, got2_hbm, got3_hbm, qgt_hbm, ot_hbm, x_hbm, c_hbm,
    wq_hbm, wk_hbm, wv_hbm, right_hbm, left_hbm, hold_hbm, stay_hbm, mine_hbm, other_hbm,
    own_s, sib_s, got2_s, got3_s, qgt_s, ot_s, x_s, c_s, wq_s, wk_s, wv_s,
    part_s, kvg_s, g_s, in_sems, out_sems,
):
    core = at_ref[0]
    fetch, store = Copies(in_sems), Copies(out_sems)

    def halves(source, target):
        count = source.shape[0] // 2
        return [
            fetch.start(row_block(source, i, count), row_block(target, i, count)) for i in range(2)
        ]

    def wait(*copies):
        for copy in copies:
            copy.wait()

    ot = halves(ot_hbm, ot_s)
    c = halves(c_hbm, c_s)
    qgt = halves(qgt_hbm, qgt_s)
    x = halves(x_hbm, x_s)
    got = halves(got2_hbm, got2_s) + halves(got3_hbm, got3_s)
    sib = halves(sib_hbm, sib_s)
    own = halves(own_hbm, own_s)
    wq, wk, wv = halves(wq_hbm, wq_s), halves(wk_hbm, wk_s), halves(wv_hbm, wv_s)
    stores = []

    def finish(index, grad_t):
        g_s[index] = grad_t.astype(bf16).T.reshape(32, 2, 16, COLS)
        rows = pl.ds(index * 16, 16)
        stores.append(store.start(g_s.at[index, :, 1 - core], other_hbm.at[:, rows]))
        stores.append(store.start(g_s.at[index, :, core], mine_hbm.at[:, rows]))

    wait(*ot, *c)
    finish(0, dot_nn(ot_s[...], c_s[...]))
    wait(*qgt, *x)
    finish(1, dot_nn(qgt_s[...], x_s[...]))
    wait(*got, *sib)
    spread2 = run_matrix(SPAN, SPAN >> 1, 1, True)
    spread4 = run_matrix(SPAN, SPAN >> 2, 2, True)
    spread8 = run_matrix(SPAN, SPAN >> 3, 3, True)
    for half in range(2):
        own[half].wait()
        rows = slice(half * SPAN, (half + 1) * SPAN)
        total = own_s[rows] + split_product(spread2, sib_s[half * 256 : half * 256 + 256])
        total = total + dot_nn(spread4, got2_s[half * 128 : half * 128 + 128])
        total = total + dot_nn(spread8, got3_s[half * 64 : half * 64 + 64])
        kvg_s[rows] = total.astype(bf16)
    for index in range(2):
        finish(2 + index, dot_nn(kvg_s[:, index * COLS : (index + 1) * COLS].T, x_s[...]))
    wait(*wq, *wk, *wv)
    outs = (right_hbm, left_hbm, hold_hbm, stay_hbm)
    for half in range(2):
        rows = slice(half * SPAN, (half + 1) * SPAN)
        grads = jnp.concatenate([qgt_s[:, rows].T, kvg_s[rows]], axis=1)
        for index, (offset, out) in enumerate(zip(ring_columns(half), outs)):
            cols = column_group(at_ref[1], offset)
            weights = jnp.concatenate([wq_s[cols, :], wk_s[cols, :], wv_s[cols, :]], axis=1)
            part = dot_nt(grads, weights)
            part_s[index, rows] = part.astype(bf16)
            stores.append(
                store.start(part_s.at[index, pl.ds(half * SPAN, SPAN)], row_block(out, half, SPAN))
            )
    wait(*stores)


def tail(at, *operands):
    dims = [operand.shape for operand in operands]
    return pl.pallas_call(
        tail_kernel,
        in_specs=[pl.BlockSpec(memory_space=pltpu.SMEM)] + [any_spec()] * len(operands),
        out_specs=[any_spec()] * 6,
        out_shape=[shape((ROWS, COLS))] * 4 + [shape((32, 64, COLS))] * 2,
        scratch_shapes=[pltpu.VMEM(o.shape, o.dtype) for o in operands]
        + [
            pltpu.VMEM((4, ROWS, COLS), bf16),
            pltpu.VMEM((ROWS, 2 * COLS), bf16),
            pltpu.VMEM((4, 32, 2, 16, COLS), bf16),
            pltpu.SemaphoreType.DMA((2 * len(dims),)),
            pltpu.SemaphoreType.DMA((16,)),
        ],
        compiler_params=params(60),
        cost_estimate=cost(7 * ROWS * WIDTH * COLS, 14 * MIB),
        name="tail",
    )(at, *operands)


def stage_kernel(at_ref, *refs, terms, picks):
    total_s = refs[-1]
    total_s[...] = sum(ref[...].astype(f32) for ref in refs[:terms]).astype(bf16)
    for pick, ref in zip(picks, refs[terms:-1]):
        for block, source in enumerate(pick(at_ref)):
            ref[block] = total_s[source]


def stage(at, terms, picks, counts, name):
    vmem = pl.BlockSpec(memory_space=pltpu.VMEM)
    dims = terms[0].shape
    return pl.pallas_call(
        functools.partial(stage_kernel, terms=len(terms), picks=picks),
        in_specs=[pl.BlockSpec(memory_space=pltpu.SMEM)] + [vmem] * len(terms),
        out_specs=[vmem] * len(counts),
        out_shape=[shape((count, *dims[1:])) for count in counts],
        scratch_shapes=[pltpu.VMEM(dims, bf16)],
        compiler_params=params(24),
        name=name,
    )(at, *terms)


def x_blocks(offset, first, count):
    return lambda at: [((at[2] + offset) & 3) * 8 + first + block for block in range(count)]


def moved(value, by):
    size = lax.axis_size("seq")
    return lax.ppermute(value, "seq", [(i, (i + by) % size) for i in range(size)])


def core_sum(at, mine, got):
    return stage(
        at,
        (mine, got),
        [x_blocks(2, 0, 4), x_blocks(2, 4, 4), x_blocks(1, 0, 8), x_blocks(3, 0, 8)]
        + [x_blocks(0, 0, 8)],
        [4, 4, 8, 8, 8],
        "sum_cores",
    )


def x_first(far_a, far_b, ahead, behind):
    got_a, got_b = moved(far_a, 16), moved(far_b, -16)
    ahead = jnp.concatenate([add(ahead[:4], got_a), ahead[4:]], axis=0)
    behind = jnp.concatenate([behind[:4], add(behind[4:], got_b)], axis=0)
    return ahead, behind


def z_sum(blocks):
    size = lax.axis_size("seq")
    along_z = [list(range(16 * x + core, 16 * x + 16, 2)) for x in range(size // 16) for core in range(2)]
    blocks = lax.all_to_all(blocks, "seq", 0, 0, axis_index_groups=along_z)
    return jnp.sum(blocks.astype(f32), axis=0)


def on_device(tokens, cotangent, w_query, w_key, w_value, w_out):
    place = lax.axis_index("seq")
    at = jnp.stack([place % 2, lax.axis_index("head"), place // 16]).astype(jnp.int32)
    key_value, own_2, own_4, own_8, queries = project_tokens(tokens, w_key, w_value, w_query)
    three_a = swapped(own_8, 2)
    level_two = swapped(own_4, 1)
    d_attended = project_cotangent(cotangent, w_out)
    d_attended, three_a = lax.optimization_barrier((d_attended, three_a))
    three_b = swapped(three_a, 1)
    entries = (key_value, own_2, level_two, three_a, three_b)
    attended_t, stats, query_part, grad_2, grad_3a, grad_3b = attend(
        entries, queries, d_attended
    )
    got_2 = swapped(grad_2, 1)
    got_3b = swapped(grad_3b, 1)
    out_parts = project_out(at, attended_t, w_out)
    out_got = head_sum_first(*out_parts)
    grad_3 = add(grad_3a, got_3b)
    near = (key_value, own_2, queries, d_attended, stats, query_part)
    near, out_parts, grad_3 = lax.optimization_barrier((near, out_parts, grad_3))
    got_3 = swapped(grad_3, 2)
    near = near_grads(*near)
    near, out_got = lax.optimization_barrier((near, out_got))
    out_more = head_sum_third(*head_sum_second(*out_got, *out_parts))
    query_grad_t, own, sibling = near
    *parts, mine, other = tail(
        at, own, sibling, got_2, got_3, query_grad_t, attended_t, tokens, cotangent,
        w_query, w_key, w_value,
    )
    (parts, mine, other), out_more = lax.optimization_barrier(((parts, mine, other), out_more))
    layer_out = head_sum_last(*out_more, *out_got, *out_parts)
    got = head_sum_first(*parts)
    far_a, far_b, ahead, behind, here = core_sum(at, mine, swapped(other, 1))
    ahead, behind = x_first(far_a, far_b, ahead, behind)
    moved_blocks = moved(ahead, 16), moved(behind, -16)
    got, _ = lax.optimization_barrier((got, (ahead, behind)))
    more = head_sum_second(*got, *parts)
    moved_blocks, _ = lax.optimization_barrier((moved_blocks, more))
    more = head_sum_third(*more)
    summed = z_sum(add(here, *moved_blocks))
    grad_tokens = head_sum_last(*more, *got, *parts)
    scale = 1.0 / math.sqrt(lax.axis_size("seq") * tokens.shape[0])
    summed = summed * scale
    return (
        layer_out,
        grad_tokens,
        summed[16:32],
        summed[32:48],
        summed[48:],
        summed[:16].T,
    )


def solution(mesh):
    return jax.shard_map(
        on_device,
        mesh=mesh,
        in_specs=(
            P("seq", None),
            P("seq", None),
            P(None, "head"),
            P(None, "head"),
            P(None, "head"),
            P("head", None),
        ),
        out_specs=(
            P("seq", "head"),
            P("seq", "head"),
            P("seq", "head"),
            P("seq", "head"),
            P("seq", "head"),
            P("head", "seq"),
        ),
        check_vma=False,
    )
```

```python
import functools
import math

import jax
import jax.numpy as jnp
from jax import lax
from jax.experimental import pallas as pl
from jax.experimental.pallas import tpu as pltpu
from jax.sharding import PartitionSpec as P

HEAD_DIM = 64
BLOCK = 256
SPAN = 2 * BLOCK
KEYS = 5 * BLOCK
ROWS = 4 * BLOCK
WIDTH = 1024
COLS = 256
MIB = 1024 * 1024
OFFSETS = (0.0, 0.0, 1.0, 2.0, 3.0)
SCORE_SCALE = 1.0 / (math.log(2.0) * math.sqrt(HEAD_DIM))
INV_ROOT = 1.0 / math.sqrt(HEAD_DIM)
bf16 = jnp.bfloat16
f32 = jnp.float32


def dot_nn(a, b):
    return lax.dot_general(a, b, (((1,), (0,)), ((), ())), preferred_element_type=f32)


def dot_nt(a, b):
    return lax.dot_general(a, b, (((1,), (1,)), ((), ())), preferred_element_type=f32)


def params(mib):
    return pltpu.CompilerParams(vmem_limit_bytes=mib * MIB)


def shape(dims, dtype=bf16):
    return jax.ShapeDtypeStruct(dims, dtype)


def cost(macs, nbytes):
    return pl.CostEstimate(flops=2 * macs, bytes_accessed=nbytes, transcendentals=0)


def run_matrix(rows, cols, shift, expand):
    i = lax.broadcasted_iota(jnp.int32, (rows, cols), 0)
    j = lax.broadcasted_iota(jnp.int32, (rows, cols), 1)
    inside = (i >> shift) == j if expand else i == (j >> shift)
    return jnp.where(inside, 2.0**-shift, 0.0).astype(bf16)


class Copies:
    def __init__(self, sems):
        self.sems = sems
        self.count = 0

    def start(self, source, target):
        copy = pltpu.make_async_copy(source, target, self.sems.at[self.count])
        self.count += 1
        copy.start()
        return copy


def row_block(ref, index, count):
    return ref.at[pl.ds(index * count, count)]


def any_spec():
    return pl.BlockSpec(memory_space=pl.ANY)


def tokens_kernel(
    x_hbm, wk_hbm, wv_hbm, wq_hbm, kv_hbm, c2_hbm, c4_hbm, c8_hbm, q_hbm,
    x_s, wk_s, wv_s, wq_s, kv_s, c2_s, c4_s, c8_s, q_s, in_sems, out_sems,
):
    fetch, store = Copies(in_sems), Copies(out_sems)
    wk = [fetch.start(row_block(wk_hbm, i, SPAN), row_block(wk_s, i, SPAN)) for i in range(2)]
    x = [fetch.start(row_block(x_hbm, i, BLOCK), row_block(x_s, i, BLOCK)) for i in range(2)]
    wv = [fetch.start(row_block(wv_hbm, i, SPAN), row_block(wv_s, i, SPAN)) for i in range(2)]
    x += [fetch.start(row_block(x_hbm, i, BLOCK), row_block(x_s, i, BLOCK)) for i in (2, 3)]
    wq = [fetch.start(row_block(wq_hbm, i, SPAN), row_block(wq_s, i, SPAN)) for i in range(2)]
    averages = [run_matrix(BLOCK >> shift, BLOCK, shift, False) for shift in range(4)]
    stores = []
    for half in range(2):
        if half == 0:
            for copy in wk:
                copy.wait()
        for copy in x[2 * half : 2 * half + 2]:
            copy.wait()
        rows = slice(half * SPAN, (half + 1) * SPAN)
        kv_s[rows, :COLS] = dot_nn(x_s[rows], wk_s[...]).astype(bf16)
        if half == 0:
            for copy in wv:
                copy.wait()
        kv_s[rows, COLS:] = dot_nn(x_s[rows], wv_s[...]).astype(bf16)
        stores.append(store.start(row_block(kv_s, half, SPAN), row_block(kv_hbm, half, SPAN)))
        for shift, ref, out in ((3, c8_s, c8_hbm), (2, c4_s, c4_hbm), (1, c2_s, c2_hbm)):
            count = BLOCK >> shift
            for index in (2 * half, 2 * half + 1):
                kv = kv_s[index * BLOCK : (index + 1) * BLOCK]
                mean = dot_nn(averages[shift], kv).astype(bf16)
                ref[index * count : (index + 1) * count] = mean
            stores.append(
                store.start(row_block(ref, half, 2 * count), row_block(out, half, 2 * count))
            )
    for copy in wq:
        copy.wait()
    for half in range(2):
        rows = slice(half * SPAN, (half + 1) * SPAN)
        q_s[rows] = dot_nn(x_s[rows], wq_s[...]).astype(bf16)
        stores.append(store.start(row_block(q_s, half, SPAN), row_block(q_hbm, half, SPAN)))
    for copy in stores:
        copy.wait()


def project_tokens(tokens, w_key, w_value, w_query):
    outs = [(ROWS >> s, 2 * COLS) for s in range(4)] + [(ROWS, COLS)]
    return pl.pallas_call(
        tokens_kernel,
        in_specs=[any_spec()] * 4,
        out_specs=[any_spec()] * 5,
        out_shape=[shape(dims) for dims in outs],
        scratch_shapes=[pltpu.VMEM((ROWS, WIDTH), bf16)]
        + [pltpu.VMEM((WIDTH, COLS), bf16)] * 3
        + [pltpu.VMEM(dims, bf16) for dims in outs]
        + [pltpu.SemaphoreType.DMA((10,)), pltpu.SemaphoreType.DMA((10,))],
        compiler_params=params(60),
        cost_estimate=cost(ROWS * WIDTH * 3 * COLS, 7 * MIB),
        name="project_tokens",
    )(tokens, w_key, w_value, w_query)


def cotangent_kernel(c_hbm, wo_hbm, da_hbm, c_s, wo_s, da_s, in_sems, out_sems):
    fetch, store = Copies(in_sems), Copies(out_sems)
    wo = [fetch.start(row_block(wo_hbm, i, 128), row_block(wo_s, i, 128)) for i in range(2)]
    c = [fetch.start(row_block(c_hbm, i, BLOCK), row_block(c_s, i, BLOCK)) for i in range(4)]
    for copy in wo:
        copy.wait()
    stores = []
    for half in range(2):
        for copy in c[2 * half : 2 * half + 2]:
            copy.wait()
        rows = slice(half * SPAN, (half + 1) * SPAN)
        da_s[rows] = dot_nt(c_s[rows], wo_s[...]).astype(bf16)
        stores.append(store.start(row_block(da_s, half, SPAN), row_block(da_hbm, half, SPAN)))
    for copy in stores:
        copy.wait()


def project_cotangent(cotangent, w_out):
    return pl.pallas_call(
        cotangent_kernel,
        in_specs=[any_spec()] * 2,
        out_specs=any_spec(),
        out_shape=shape((ROWS, COLS)),
        scratch_shapes=[
            pltpu.VMEM((ROWS, WIDTH), bf16),
            pltpu.VMEM((COLS, WIDTH), bf16),
            pltpu.VMEM((ROWS, COLS), bf16),
            pltpu.SemaphoreType.DMA((6,)),
            pltpu.SemaphoreType.DMA((2,)),
        ],
        compiler_params=params(60),
        cost_estimate=cost(ROWS * WIDTH * COLS, 4 * MIB),
        name="project_cotangent",
    )(cotangent, w_out)


def entry_rows(refs, kb, lo):
    near, c2, l2, l3a, l3b = refs
    if kb < 2:
        return near[kb * BLOCK : (kb + 1) * BLOCK, lo : lo + 128]
    if kb == 2:
        return c2[:, lo : lo + 128]
    if kb == 3:
        return l2[:, lo : lo + 128]
    return jnp.concatenate([l3a[:, lo : lo + 128], l3b[:, lo : lo + 128]], axis=0)


def only_head(ref, head):
    lane = lax.broadcasted_iota(jnp.int32, (SPAN, 128), 1)
    keep = lane < HEAD_DIM if head % 2 == 0 else lane >= HEAD_DIM
    pair = head // 2 * 128
    return jnp.where(keep, ref[:, pair : pair + 128], jnp.zeros((), bf16))


def fold(values, combine):
    return combine(values.reshape(BLOCK // 8, 8, SPAN), axis=0)


def forward_kernel(*refs):
    entries, q_ref, da_ref, at_ref, wo_ref = refs[:5], *refs[5:9]
    ot_ref, stat_ref, qgt_ref, g2_ref, g3a_ref, g3b_ref = refs[9:15]
    out_refs = refs[15:19]
    w_s, vt_s, kt_s, qm_s, dm_s, grad_s = refs[19:]
    step = pl.program_id(0)
    for kb in range(5):
        rows = slice(kb * BLOCK, (kb + 1) * BLOCK)
        for pair in range(2):
            lanes = slice(pair * 128, pair * 128 + 128)
            vt_s[lanes, rows] = entry_rows(entries, kb, COLS + pair * 128).T
            if kb >= 3:
                key = entry_rows(entries, kb, pair * 128)
                kt_s[lanes, (kb - 3) * BLOCK : (kb - 2) * BLOCK] = key.T
    for head in range(4):
        qm_s[head] = only_head(q_ref, head)
        dm_s[head] = only_head(da_ref, head)

    @pl.when(step == 0)
    def _():
        grad_s[...] = jnp.zeros_like(grad_s)

    for pair in range(2):
        lo = pair * 128
        key_grad = value_grad = 0.0
        keys, values = [
            jnp.concatenate([entry_rows(entries, kb, first + lo) for kb in range(5)], axis=0)
            for first in (0, COLS)
        ]
        for side in range(2):
            head = 2 * pair + side
            t = dot_nt(keys, qm_s[head])
            p = dot_nt(values, dm_s[head])
            tops = []
            for kb in range(5):
                rows = slice(kb * BLOCK, (kb + 1) * BLOCK)
                tops.append(fold(t[rows], jnp.max) * SCORE_SCALE + OFFSETS[kb])
            top = jnp.max(functools.reduce(jnp.maximum, tops), axis=0, keepdims=True)
            total = inner = jnp.zeros((8, SPAN), f32)
            far = []
            for kb in range(5):
                rows = slice(kb * BLOCK, (kb + 1) * BLOCK)
                raised = jnp.exp2(t[rows] * SCORE_SCALE + (OFFSETS[kb] - top))
                w_s[side, rows] = raised.astype(bf16)
                total = total + fold(raised, jnp.sum)
                inner = inner + fold(raised * p[rows], jnp.sum)
                if kb >= 3:
                    far.append((raised, p[rows]))
            total = jnp.sum(total, axis=0, keepdims=True)
            inverse = 1.0 / total
            inner = jnp.sum(inner, axis=0, keepdims=True) * inverse
            mine = slice(head * HEAD_DIM, (head + 1) * HEAD_DIM)
            ot_ref[mine] = (dot_nn(vt_s[mine, :], w_s[side]) * inverse).astype(bf16)
            stat_ref[head : head + 1] = top + jnp.log2(total)
            stat_ref[head + 4 : head + 5] = inner
            weights, scores = [], []
            for raised, p_far in far:
                attention = raised * inverse
                weights.append(attention.astype(bf16))
                scores.append((attention * (p_far - inner)).astype(bf16))
            weights, scores = jnp.concatenate(weights, axis=0), jnp.concatenate(scores, axis=0)
            qgt_ref[mine] = dot_nn(kt_s[mine, :], scores)
            key_grad = key_grad + dot_nn(scores, qm_s[head])
            value_grad = value_grad + dot_nn(weights, dm_s[head])
        grad_s[:, lo : lo + 128] += key_grad
        grad_s[:, COLS + lo : COLS + lo + 128] += value_grad

    attended = ot_ref[...].T
    for first, second, ref in zip(ring_columns(0), ring_columns(1), out_refs):
        cols = column_group(at_ref[1], jnp.where(step == 0, first, second))
        ref[...] = dot_nn(attended, wo_ref[:, cols]).astype(bf16)

    @pl.when(step == 1)
    def _():
        for ref, first, count in ((g2_ref, 0, 256), (g3a_ref, 256, 128), (g3b_ref, 384, 128)):
            rows = slice(first, first + count)
            ref[:, :COLS] = (grad_s[rows, :COLS] * INV_ROOT).astype(bf16)
            ref[:, COLS:] = grad_s[rows, COLS:].astype(bf16)


def attend(entries, queries, d_attended, at, w_out):
    part = pl.BlockSpec((SPAN, COLS), lambda i: (i, 0))
    turned = pl.BlockSpec((COLS, SPAN), lambda i: (0, i))
    two = pl.BlockSpec((BLOCK, 2 * COLS), lambda i: (0, 0))
    three = pl.BlockSpec((BLOCK // 2, 2 * COLS), lambda i: (0, 0))
    return pl.pallas_call(
        forward_kernel,
        grid=(2,),
        in_specs=[
            pl.BlockSpec((SPAN, 2 * COLS), lambda i: (i, 0)),
            pl.BlockSpec((BLOCK, 2 * COLS), lambda i: (1 - i, 0)),
            two,
            three,
            three,
            part,
            part,
            pl.BlockSpec(memory_space=pltpu.SMEM),
            pl.BlockSpec((COLS, WIDTH), lambda i: (0, 0)),
        ],
        out_specs=[turned, pl.BlockSpec((8, SPAN), lambda i: (0, i)), turned, two, three, three]
        + [part] * 4,
        out_shape=[
            shape((COLS, ROWS)),
            shape((8, ROWS), f32),
            shape((COLS, ROWS), f32),
            shape((BLOCK, 2 * COLS)),
            shape((BLOCK // 2, 2 * COLS)),
            shape((BLOCK // 2, 2 * COLS)),
        ]
        + [shape((ROWS, COLS))] * 4,
        scratch_shapes=[
            pltpu.VMEM((2, KEYS, SPAN), bf16),
            pltpu.VMEM((COLS, KEYS), bf16),
            pltpu.VMEM((COLS, 2 * BLOCK), bf16),
            pltpu.VMEM((4, SPAN, 128), bf16),
            pltpu.VMEM((4, SPAN, 128), bf16),
            pltpu.VMEM((2 * BLOCK, 2 * COLS), f32),
        ],
        compiler_params=params(60),
        cost_estimate=cost(4 * 4 * 4 * ROWS * KEYS * 64, 6 * MIB),
        name="attend",
    )(*entries, queries, d_attended, at, w_out)


def block_grads(key_rows, value_rows, keys_t, offsets, qm, dm, stat, inner):
    t = dot_nt(key_rows, qm) * SCORE_SCALE
    p = dot_nt(value_rows, dm)
    weights, scores = [], []
    for index, offset in enumerate(offsets):
        rows = slice(index * BLOCK, (index + 1) * BLOCK)
        attention = jnp.exp2(t[rows] + (offset - stat))
        weights.append(attention.astype(bf16))
        scores.append((attention * (p[rows] - inner)).astype(bf16))
    weights, scores = jnp.concatenate(weights, axis=0), jnp.concatenate(scores, axis=0)
    return dot_nn(keys_t, scores), dot_nn(scores, qm), dot_nn(weights, dm)


def near_kernel(near, c2, q_ref, da_ref, stat_ref, part_ref, qgt_ref, own_ref, sib_ref,
                kt_s, qm_s, dm_s):
    refs = (near, c2, None, None, None)
    for kb in range(3):
        rows = slice(kb * BLOCK, (kb + 1) * BLOCK)
        for pair in range(2):
            part = entry_rows(refs, kb, pair * 128)
            kt_s[pair * 128 : pair * 128 + 128, rows] = part.T
    for head in range(4):
        qm_s[head] = only_head(q_ref, head)
        dm_s[head] = only_head(da_ref, head)
    for pair in range(2):
        lo = pair * 128
        key_grad = value_grad = 0.0
        stack = [
            jnp.concatenate([entry_rows(refs, kb, first + lo) for kb in range(3)], axis=0)
            for first in (0, COLS)
        ]
        for side in range(2):
            head = 2 * pair + side
            mine = slice(head * HEAD_DIM, (head + 1) * HEAD_DIM)
            dq, dk, dv = block_grads(
                *stack, kt_s[mine, :], OFFSETS[:3], qm_s[head], dm_s[head],
                stat_ref[head : head + 1], stat_ref[head + 4 : head + 5],
            )
            qgt_ref[mine] = ((part_ref[mine] + dq) * INV_ROOT).astype(bf16)
            key_grad, value_grad = key_grad + dk, value_grad + dv
        key_grad = key_grad * INV_ROOT
        own_ref[:, lo : lo + 128] = key_grad[:SPAN]
        own_ref[:, COLS + lo : COLS + lo + 128] = value_grad[:SPAN]
        sib_ref[:, lo : lo + 128] = key_grad[SPAN:]
        sib_ref[:, COLS + lo : COLS + lo + 128] = value_grad[SPAN:]


def near_grads(key_value, own_2, queries, d_attended, stats, query_part):
    part = pl.BlockSpec((SPAN, COLS), lambda i: (i, 0))
    turned = pl.BlockSpec((COLS, SPAN), lambda i: (0, i))
    near = pl.BlockSpec((SPAN, 2 * COLS), lambda i: (i, 0))
    sibling = pl.BlockSpec((BLOCK, 2 * COLS), lambda i: (1 - i, 0))
    return pl.pallas_call(
        near_kernel,
        grid=(2,),
        in_specs=[near, sibling, part, part, pl.BlockSpec((8, SPAN), lambda i: (0, i)), turned],
        out_specs=[turned, near, sibling],
        out_shape=[
            shape((COLS, ROWS)),
            shape((ROWS, 2 * COLS), f32),
            shape((SPAN, 2 * COLS), f32),
        ],
        scratch_shapes=[
            pltpu.VMEM((COLS, 3 * BLOCK), bf16),
            pltpu.VMEM((4, SPAN, 128), bf16),
            pltpu.VMEM((4, SPAN, 128), bf16),
        ],
        compiler_params=params(60),
        cost_estimate=cost(4 * 5 * 4 * ROWS * 3 * BLOCK * 64, 8 * MIB),
        name="near_grads",
    )(key_value, own_2, queries, d_attended, stats, query_part)


def split_product(matrix, values):
    high = values.astype(bf16)
    low = (values - high.astype(f32)).astype(bf16)
    return dot_nn(matrix, high) + dot_nn(matrix, low)


def ring_columns(half):
    return (2, 3, 1, 0) if half == 0 else (1, 2, 3, 0)


def column_group(here, offset):
    return pl.ds(pl.multiple_of(((here + offset) & 3) * COLS, COLS), COLS)


def shifted(value, by):
    size = lax.axis_size("head")
    return lax.ppermute(value, "head", [(i, (i + by) % size) for i in range(size)])


def swapped(value, bits):
    return lax.ppermute(value, "seq", [(i, i ^ bits) for i in range(lax.axis_size("seq"))])


def add(*terms):
    return sum(term.astype(f32) for term in terms).astype(bf16)


def head_sum_first(right, left, hold, mine):
    return shifted(right, 1), shifted(left, -1)


def head_sum_second(got_right, got_left, right, left, hold, mine):
    half = ROWS // 2
    return add(hold[:half], got_right[:half]), add(hold[half:], got_left[half:])


def head_sum_third(more_right, more_left):
    return shifted(more_right, 1), shifted(more_left, -1)


def head_sum_last(more_right, more_left, got_right, got_left, right, left, hold, mine):
    half = ROWS // 2
    return jnp.concatenate(
        [
            add(mine[:half], got_left[:half], more_right),
            add(mine[half:], got_right[half:], more_left),
        ],
        axis=0,
    )


def tail_kernel(
    at_ref, own_hbm, sib_hbm, got2_hbm, got3_hbm, qgt_hbm, ot_hbm, x_hbm, c_hbm,
    wq_hbm, wk_hbm, wv_hbm, right_hbm, left_hbm, hold_hbm, stay_hbm, mine_hbm, other_hbm,
    own_s, sib_s, got2_s, got3_s, qgt_s, ot_s, x_s, c_s, wq_s, wk_s, wv_s,
    part_s, kvg_s, g_s, in_sems, out_sems,
):
    core = at_ref[0]
    fetch, store = Copies(in_sems), Copies(out_sems)

    def halves(source, target):
        count = source.shape[0] // 2
        return [
            fetch.start(row_block(source, i, count), row_block(target, i, count)) for i in range(2)
        ]

    def wait(*copies):
        for copy in copies:
            copy.wait()

    ot = halves(ot_hbm, ot_s)
    c = halves(c_hbm, c_s)
    qgt = halves(qgt_hbm, qgt_s)
    x = halves(x_hbm, x_s)
    got = halves(got2_hbm, got2_s) + halves(got3_hbm, got3_s)
    sib = halves(sib_hbm, sib_s)
    own = halves(own_hbm, own_s)
    wq, wk, wv = halves(wq_hbm, wq_s), halves(wk_hbm, wk_s), halves(wv_hbm, wv_s)
    stores = []

    def finish(index, grad_t):
        g_s[index] = grad_t.astype(bf16).T.reshape(32, 2, 16, COLS)
        rows = pl.ds(index * 16, 16)
        stores.append(store.start(g_s.at[index, :, 1 - core], other_hbm.at[:, rows]))
        stores.append(store.start(g_s.at[index, :, core], mine_hbm.at[:, rows]))

    wait(*ot, *c)
    finish(0, dot_nn(ot_s[...], c_s[...]))
    wait(*qgt, *x)
    finish(1, dot_nn(qgt_s[...], x_s[...]))
    wait(*got, *sib)
    spread2 = run_matrix(SPAN, SPAN >> 1, 1, True)
    spread4 = run_matrix(SPAN, SPAN >> 2, 2, True)
    spread8 = run_matrix(SPAN, SPAN >> 3, 3, True)
    for half in range(2):
        own[half].wait()
        rows = slice(half * SPAN, (half + 1) * SPAN)
        total = own_s[rows] + split_product(spread2, sib_s[half * 256 : half * 256 + 256])
        total = total + dot_nn(spread4, got2_s[half * 128 : half * 128 + 128])
        total = total + dot_nn(spread8, got3_s[half * 64 : half * 64 + 64])
        kvg_s[rows] = total.astype(bf16)
    for index in range(2):
        finish(2 + index, dot_nn(kvg_s[:, index * COLS : (index + 1) * COLS].T, x_s[...]))
    wait(*wq, *wk, *wv)
    outs = (right_hbm, left_hbm, hold_hbm, stay_hbm)
    for half in range(2):
        rows = slice(half * SPAN, (half + 1) * SPAN)
        grads = jnp.concatenate([qgt_s[:, rows].T, kvg_s[rows]], axis=1)
        for index, (offset, out) in enumerate(zip(ring_columns(half), outs)):
            cols = column_group(at_ref[1], offset)
            weights = jnp.concatenate([wq_s[cols, :], wk_s[cols, :], wv_s[cols, :]], axis=1)
            part = dot_nt(grads, weights)
            part_s[index, rows] = part.astype(bf16)
            stores.append(
                store.start(part_s.at[index, pl.ds(half * SPAN, SPAN)], row_block(out, half, SPAN))
            )
    wait(*stores)


def tail(at, *operands):
    dims = [operand.shape for operand in operands]
    return pl.pallas_call(
        tail_kernel,
        in_specs=[pl.BlockSpec(memory_space=pltpu.SMEM)] + [any_spec()] * len(operands),
        out_specs=[any_spec()] * 6,
        out_shape=[shape((ROWS, COLS))] * 4 + [shape((32, 64, COLS))] * 2,
        scratch_shapes=[pltpu.VMEM(o.shape, o.dtype) for o in operands]
        + [
            pltpu.VMEM((4, ROWS, COLS), bf16),
            pltpu.VMEM((ROWS, 2 * COLS), bf16),
            pltpu.VMEM((4, 32, 2, 16, COLS), bf16),
            pltpu.SemaphoreType.DMA((2 * len(dims),)),
            pltpu.SemaphoreType.DMA((16,)),
        ],
        compiler_params=params(60),
        cost_estimate=cost(7 * ROWS * WIDTH * COLS, 14 * MIB),
        name="tail",
    )(at, *operands)


def stage_kernel(at_ref, *refs, terms, picks):
    total_s = refs[-1]
    total_s[...] = sum(ref[...].astype(f32) for ref in refs[:terms]).astype(bf16)
    for pick, ref in zip(picks, refs[terms:-1]):
        for block, source in enumerate(pick(at_ref)):
            ref[block] = total_s[source]


def stage(at, terms, picks, counts, name):
    vmem = pl.BlockSpec(memory_space=pltpu.VMEM)
    dims = terms[0].shape
    return pl.pallas_call(
        functools.partial(stage_kernel, terms=len(terms), picks=picks),
        in_specs=[pl.BlockSpec(memory_space=pltpu.SMEM)] + [vmem] * len(terms),
        out_specs=[vmem] * len(counts),
        out_shape=[shape((count, *dims[1:])) for count in counts],
        scratch_shapes=[pltpu.VMEM(dims, bf16)],
        compiler_params=params(24),
        name=name,
    )(at, *terms)


def x_blocks(offset, first, count):
    return lambda at: [((at[2] + offset) & 3) * 8 + first + block for block in range(count)]


def moved(value, by):
    size = lax.axis_size("seq")
    return lax.ppermute(value, "seq", [(i, (i + by) % size) for i in range(size)])


def core_sum(at, mine, got):
    return stage(
        at,
        (mine, got),
        [x_blocks(2, 0, 4), x_blocks(2, 4, 4), x_blocks(1, 0, 8), x_blocks(3, 0, 8)]
        + [x_blocks(0, 0, 8)],
        [4, 4, 8, 8, 8],
        "sum_cores",
    )


def x_first(far_a, far_b, ahead, behind):
    got_a, got_b = moved(far_a, 16), moved(far_b, -16)
    ahead = jnp.concatenate([add(ahead[:4], got_a), ahead[4:]], axis=0)
    behind = jnp.concatenate([behind[:4], add(behind[4:], got_b)], axis=0)
    return ahead, behind


def z_sum(blocks):
    size = lax.axis_size("seq")
    along_z = [list(range(16 * x + core, 16 * x + 16, 2)) for x in range(size // 16) for core in range(2)]
    blocks = lax.all_to_all(blocks, "seq", 0, 0, axis_index_groups=along_z)
    return jnp.sum(blocks.astype(f32), axis=0)


def on_device(tokens, cotangent, w_query, w_key, w_value, w_out):
    place = lax.axis_index("seq")
    at = jnp.stack([place % 2, lax.axis_index("head"), place // 16]).astype(jnp.int32)
    key_value, own_2, own_4, own_8, queries = project_tokens(tokens, w_key, w_value, w_query)
    three_a = swapped(own_8, 2)
    level_two = swapped(own_4, 1)
    d_attended = project_cotangent(cotangent, w_out)
    d_attended, three_a = lax.optimization_barrier((d_attended, three_a))
    three_b = swapped(three_a, 1)
    entries = (key_value, own_2, level_two, three_a, three_b)
    attended_t, stats, query_part, grad_2, grad_3a, grad_3b, *out_parts = attend(
        entries, queries, d_attended, at, w_out
    )
    got_2 = swapped(grad_2, 1)
    got_3b = swapped(grad_3b, 1)
    out_got = head_sum_first(*out_parts)
    grad_3 = add(grad_3a, got_3b)
    near = (key_value, own_2, queries, d_attended, stats, query_part)
    near, out_parts, grad_3 = lax.optimization_barrier((near, out_parts, grad_3))
    got_3 = swapped(grad_3, 2)
    near = near_grads(*near)
    near, out_got = lax.optimization_barrier((near, out_got))
    out_more = head_sum_third(*head_sum_second(*out_got, *out_parts))
    query_grad_t, own, sibling = near
    *parts, mine, other = tail(
        at, own, sibling, got_2, got_3, query_grad_t, attended_t, tokens, cotangent,
        w_query, w_key, w_value,
    )
    (parts, mine, other), out_more = lax.optimization_barrier(((parts, mine, other), out_more))
    layer_out = head_sum_last(*out_more, *out_got, *out_parts)
    got = head_sum_first(*parts)
    far_a, far_b, ahead, behind, here = core_sum(at, mine, swapped(other, 1))
    ahead, behind = x_first(far_a, far_b, ahead, behind)
    moved_blocks = moved(ahead, 16), moved(behind, -16)
    got, _ = lax.optimization_barrier((got, (ahead, behind)))
    more = head_sum_second(*got, *parts)
    moved_blocks, _ = lax.optimization_barrier((moved_blocks, more))
    more = head_sum_third(*more)
    summed = z_sum(add(here, *moved_blocks))
    grad_tokens = head_sum_last(*more, *got, *parts)
    scale = 1.0 / math.sqrt(lax.axis_size("seq") * tokens.shape[0])
    summed = summed * scale
    return (
        layer_out,
        grad_tokens,
        summed[16:32],
        summed[32:48],
        summed[48:],
        summed[:16].T,
    )


def solution(mesh):
    return jax.shard_map(
        on_device,
        mesh=mesh,
        in_specs=(
            P("seq", None),
            P("seq", None),
            P(None, "head"),
            P(None, "head"),
            P(None, "head"),
            P("head", None),
        ),
        out_specs=(
            P("seq", "head"),
            P("seq", "head"),
            P("seq", "head"),
            P("seq", "head"),
            P("seq", "head"),
            P("head", "seq"),
        ),
        check_vma=False,
    )
```
